128 devices in a mesh: seq: 8 (over x_lo, y), exp: 16 (over x_hi, z, core).
Axes of the slice: x: 4 (x_hi: 2, x_lo: 2; x = x_hi * 2 + x_lo), y: 4, z: 4, core: 2. Of those that a mesh axis runs over, the one named last changes fastest.
Arguments:
- frames: bfloat16 [16, 1024, 1536], P('exp', 'seq'), may hold values from -6 to 6
- conv_weight: float32 [31, 1536], replicated, may hold values from -1 to 1
- gate_probs: float32 [16, 1024, 2], P('exp', 'seq'), may hold values from 0.1 to 1
- expert_ids: int32 [16, 1024, 2], P('exp', 'seq'), may hold values from 0 to 31, all different within a row; in each aligned block of 128 rows (0 to 127, 128 to 255, ..., all dimensions but the last counted through in order) at most 16 rows name the same one
- lengths: int32 [16], P('exp'), may hold values from 256 to 1024, as said below
- placement: int32 [32], replicated, may hold values from 0 to 31, each once
- weight_in: bfloat16 [32, 1536, 6144], P('exp', None, 'seq'), may hold values from -0.15625 to 0.15625
- weight_out: bfloat16 [32, 6144, 1536], P('exp', 'seq'), may hold values from -0.078125 to 0.078125
- cotangent: bfloat16 [16, 1024, 1536], P('exp', 'seq'), may hold values from -6 to 6
Outputs:
- block_out: bfloat16 [16, 1024, 1536], P('exp', 'seq')
- d_frames: bfloat16 [16, 1024, 1536], P('exp', 'seq')
- d_gate_probs: float32 [16, 1024, 2], P('exp', 'seq')
- d_conv_weight: float32 [31, 1536], replicated
- d_weight_in: bfloat16 [32, 1536, 6144], P('exp', None, 'seq')
- d_weight_out: bfloat16 [32, 6144, 1536], P('exp', 'seq')
The draws below stay inside these ranges and needn't reach their ends.
Inputs may be any that keep to these rules, and one draw needn't show every extreme that they name: `expert_ids`: each row names 2 different experts; in each aligned block of 128 frames of a group no expert is named by more than 16 rows. `lengths`: some group has all 1024 frames live. `placement`: each weight slot serves exactly one expert.
All inputs are finite; a program needn't handle non-finite values.
Results may differ from the reference program's by a relative error of at most 0.013.
Values may be sent and summed in bfloat16 or wider, within the bound.
No kernel may reach another device: no remote copies, remote signals or barrier semaphores. Data moves between devices by JAX's collectives and lax.ppermute only.
A program may use at most 192 MiB of HBM per device.

```python
import math
import jax
import jax.numpy as jnp
import numpy as np
from jax import lax

D = 1536
FF = 6144
TAPS = 31
TOP = 2
FR_DEV = 128
EXPERTS = 32
CAP = 8
GROUPS = 16
LEN = 1024
N_SEQ = 8


def draw_lengths(key, part):
    key = jax.random.fold_in(key, 7)
    first_key, second_key = jax.random.split(key)
    picked = jax.random.randint(first_key, (GROUPS,), LEN // 4, LEN + 1)
    full_group = jax.random.randint(second_key, (), 0, GROUPS)
    return jnp.where(jnp.arange(GROUPS) == full_group, LEN, picked).astype(jnp.int32)


def block_scale(rng, dims, cuts, smallest, top_value):
    gain, own = 1.0, jax.random.fold_in(rng, 6)
    for axis_at, blocks in cuts:
        draws = jnp.exp(jax.random.uniform(jax.random.fold_in(own, axis_at), (blocks,), jnp.float32, smallest / len(cuts), top_value / len(cuts)))
        gain = gain * jnp.repeat(draws, dims[axis_at] // blocks).reshape([-1 if axis == axis_at else 1 for axis in range(len(dims))])
    return gain


def routed_block(stream_key, own, number, rows, amount, top, limit, lean):
    ranking = jax.random.permutation(stream_key, amount)
    crowded, common = shares(amount, rows * top, limit, lean, True), shares(amount, rows * top, limit, lean, False)
    places = jnp.arange(amount)

    def named(tallies, offset_by):
        used = int((tallies > 0).sum())
        fixed = max(1, used // 4)
        shifted = fixed + (places - fixed + offset_by * (used - fixed)) % max(1, amount - fixed)
        return jnp.zeros((amount,), jnp.int32).at[ranking[jnp.where(places < fixed, places, shifted)]].set(jnp.asarray(tallies, jnp.int32))

    tallies = jnp.where(number % 4 == 0, named(crowded, number // 4), named(common, number - number // 4 - 1))
    mixed = jax.random.permutation(jax.random.fold_in(own, 3), amount)
    source_of, receiver = mixed[0:amount // 2 * 2:2], mixed[1:amount // 2 * 2:2]
    slack = jnp.minimum(tallies[source_of] - 1, limit - tallies[receiver]) // 2
    slack = jnp.where((source_of == ranking[0]) | (receiver == ranking[0]) | (tallies[receiver] == 0), 0, jnp.maximum(slack, 0))
    shifted = jax.random.randint(jax.random.fold_in(own, 4), (amount // 2,), 0, 1 << 20) % (slack + 1)
    tallies = tallies.at[source_of].add(-shifted).at[receiver].add(shifted)
    members = jnp.searchsorted(jnp.cumsum(tallies), jnp.arange(rows * top), side="right").astype(jnp.int32)
    listing = members.reshape(top, rows).T
    listing = listing[jax.random.permutation(jax.random.fold_in(own, 1), rows)]
    offset_by = jax.random.randint(jax.random.fold_in(own, 2), (rows, 1), 0, top)
    return jnp.take_along_axis(listing, (jnp.arange(top)[None, :] + offset_by) % top, axis=1)


def shares(number_of, total, most, skew, full):
    portions = [(1 << 20) // math.isqrt(rank ** skew) + 1 for rank in range(1, number_of + 1)]
    largest = most if full else min(most, max(-(-total // number_of), total * portions[0] // sum(portions)))
    least = 1 if total - largest >= number_of - 1 else 0
    counts, surplus = [largest] + [least] * (number_of - 1), total - largest - least * (number_of - 1)
    while surplus > 0:
        free = [i for i in range(1, number_of) if counts[i] < largest] or [i for i in range(1, number_of) if counts[i] < most]
        pool, left = sum([portions[i] for i in free]), surplus
        for i in free:
            extra = min(most - counts[i], max(1, left * portions[i] // pool), surplus)
            counts[i] = counts[i] + extra
            surplus = surplus - extra
    return np.array(counts)


def scatter_about(key, dims, width, limit, cuts=(), held_as=jnp.bfloat16):
    array = jax.random.normal(key, dims, jnp.float32) * width
    if len(cuts) > 0:
        array = block_scale(key, dims, cuts, -0.22, 0.18) * array
    return jnp.clip(array, min=-limit, max=limit).astype(held_as)


def setup_inputs(seed: int = 0) -> dict:
    arg_keys = jax.random.split(jax.random.key(seed), 10)
    frames = scatter_about(arg_keys[0], (GROUPS, LEN, D), 1.0, 6.0, ((0, 16), (1, 8)))
    conv_weight = scatter_about(arg_keys[1], (TAPS, D), TAPS ** -0.5, 1.0, (), jnp.float32)
    gate_probs = jnp.clip(0.1 + 0.9 * jax.random.uniform(arg_keys[2], (GROUPS, LEN, TOP), jnp.float32) ** block_scale(arg_keys[2], (GROUPS, LEN, TOP), ((0, 16), (1, 8)), -0.2, 0.2), 0.1, 1.0)
    expert_ids_keys = jax.random.split(jax.random.fold_in(arg_keys[3], 1), GROUPS * LEN // FR_DEV)
    expert_ids_turns = jax.random.permutation(jax.random.fold_in(arg_keys[3], 3), GROUPS * LEN // FR_DEV)
    expert_ids = jax.vmap(lambda own, number: routed_block(jax.random.fold_in(arg_keys[3], 2), own, number, FR_DEV, EXPERTS, TOP, 2 * CAP, 2))(expert_ids_keys, expert_ids_turns).reshape((GROUPS, LEN, TOP))
    lengths = draw_lengths(jax.random.fold_in(arg_keys[9], 71), 0)
    placement = jax.random.permutation(arg_keys[5], EXPERTS).astype(jnp.int32)
    weight_in = scatter_about(arg_keys[6], (EXPERTS, D, FF), D ** -0.5, 0.15625, ((0, 16), (2, 8)))
    weight_out = scatter_about(arg_keys[7], (EXPERTS, FF, D), FF ** -0.5, 0.078125, ((0, 16), (1, 8)))
    cotangent = scatter_about(arg_keys[8], (GROUPS, LEN, D), 1.0, 6.0, ((0, 16), (1, 8)))
    return dict(frames=frames, conv_weight=conv_weight, gate_probs=gate_probs, expert_ids=expert_ids, lengths=lengths, placement=placement, weight_in=weight_in, weight_out=weight_out, cotangent=cotangent)


def swish_slope(value):
    sigmoid_value = jax.nn.sigmoid(value)
    return sigmoid_value + value * sigmoid_value * (1.0 - sigmoid_value)

def reference(frames, conv_weight, gate_probs, expert_ids, lengths, placement, weight_in, weight_out, cotangent):
    half_taps = (TAPS - 1) // 2
    hidden_part = FF // N_SEQ
    total_rows = GROUPS * N_SEQ * CAP
    frames_f32 = frames.astype(jnp.float32)
    inv_rms = lax.rsqrt(lax.optimization_barrier(jnp.mean(frames_f32 * frames_f32, axis=-1, keepdims=True)) + 1e-06)
    unit_rows = frames_f32 * inv_rms
    live_int = (jnp.arange(LEN, dtype=jnp.int32)[None, :] < lengths[:, None]).astype(jnp.int32)
    live_mask = live_int.astype(jnp.float32)[:, :, None]
    normed = (unit_rows * live_mask).astype(jnp.bfloat16)
    normed_wide = jnp.pad(normed.astype(jnp.float32), ((0, 0), (half_taps, half_taps), (0, 0)))
    conv_out = jnp.zeros_like(frames_f32)
    for tap_index in range(TAPS):
        conv_out = conv_out + normed_wide[:, tap_index:tap_index + LEN] * conv_weight[tap_index]
    mid_rows = (frames_f32 + live_mask * jax.nn.silu(conv_out)).astype(jnp.bfloat16)
    matches = (expert_ids[..., None] == jnp.arange(EXPERTS, dtype=jnp.int32)).astype(jnp.int32)
    counted = (matches * live_int[:, :, None, None]).reshape(GROUPS, N_SEQ, FR_DEV * TOP, EXPERTS)
    earlier = jnp.cumsum(counted, axis=2) - counted
    slot_index = lax.optimization_barrier(jnp.sum(earlier * counted, axis=-1)).reshape(GROUPS, LEN, TOP).astype(jnp.int32)
    kept_bool = (live_int[:, :, None] == 1) & (slot_index < CAP)
    kept_mask = kept_bool.astype(jnp.float32)
    slot_send = jnp.where(kept_bool, slot_index, CAP).astype(jnp.int32)
    slot_read = jnp.minimum(slot_index, CAP - 1).astype(jnp.int32)
    group_index = jnp.broadcast_to(jnp.arange(GROUPS, dtype=jnp.int32)[:, None, None], expert_ids.shape)
    block_index = jnp.broadcast_to((jnp.arange(LEN, dtype=jnp.int32) // FR_DEV)[None, :, None], expert_ids.shape)

    def pack_rows(values):
        empty_buf = jnp.zeros((EXPERTS, GROUPS, N_SEQ, CAP + 1, D), values.dtype)
        filled = empty_buf.at[expert_ids, group_index, block_index, slot_send].set(values)
        return filled[:, :, :, :CAP].reshape(EXPERTS, total_rows, D)

    def unpack_rows(buffer):
        shaped = buffer.reshape(EXPERTS, GROUPS, N_SEQ, CAP, D)
        return shaped[expert_ids, group_index, block_index, slot_read] * kept_mask[..., None]

    def block_sum(part_sums):
        rounded = lax.optimization_barrier(part_sums.astype(jnp.bfloat16))
        return lax.optimization_barrier(jnp.sum(rounded.astype(jnp.float32), axis=0))

    def forward_expert(inputs):
        rows_in, slot_of = inputs
        pre_act = jnp.dot(rows_in, weight_in[slot_of], preferred_element_type=jnp.float32)
        hidden = jax.nn.silu(pre_act).astype(jnp.bfloat16)
        part_sums = jnp.einsum('rjf,jfd->jrd', hidden.astype(jnp.float32).reshape(total_rows, N_SEQ, hidden_part), weight_out[slot_of].astype(jnp.float32).reshape(N_SEQ, hidden_part, D))
        return block_sum(part_sums)
    expert_rows = pack_rows(jnp.broadcast_to(mid_rows[:, :, None, :], (GROUPS, LEN, TOP, D)))
    out_buf = lax.map(forward_expert, (expert_rows, placement))
    expert_out = unpack_rows(out_buf)
    mix_out = lax.optimization_barrier(jnp.sum(gate_probs[..., None] * kept_mask[..., None] * expert_out, axis=2))
    block_out = (mid_rows.astype(jnp.float32) + mix_out).astype(jnp.bfloat16)
    grad_out = cotangent.astype(jnp.float32)
    d_gate_probs = kept_mask * lax.optimization_barrier(jnp.sum(grad_out[:, :, None, :] * expert_out, axis=-1))
    d_expert_out = ((gate_probs * kept_mask)[..., None] * grad_out[:, :, None, :]).astype(jnp.bfloat16)
    grad_rows = pack_rows(d_expert_out)

    def backward_expert(inputs):
        rows_in, grads_in, slot_of = inputs
        pre_act = jnp.dot(rows_in, weight_in[slot_of], preferred_element_type=jnp.float32)
        hidden = jax.nn.silu(pre_act).astype(jnp.bfloat16)
        d_hidden = jnp.dot(grads_in, weight_out[slot_of].T, preferred_element_type=jnp.float32)
        d_pre = (d_hidden * swish_slope(pre_act)).astype(jnp.bfloat16)
        grad_out_w = jnp.dot(hidden.T, grads_in, preferred_element_type=jnp.float32).astype(jnp.bfloat16)
        grad_in_w = jnp.dot(rows_in.T, d_pre, preferred_element_type=jnp.float32).astype(jnp.bfloat16)
        part_sums = jnp.einsum('rjf,djf->jrd', d_pre.astype(jnp.float32).reshape(total_rows, N_SEQ, hidden_part), weight_in[slot_of].astype(jnp.float32).reshape(D, N_SEQ, hidden_part))
        return (block_sum(part_sums), grad_in_w, grad_out_w)
    d_expert_buf, grads_in_all, grads_out_all = lax.map(backward_expert, (expert_rows, grad_rows, placement))
    d_weight_in = jnp.zeros_like(weight_in).at[placement].set(grads_in_all)
    d_weight_out = jnp.zeros_like(weight_out).at[placement].set(grads_out_all)
    d_mid = grad_out + lax.optimization_barrier(jnp.sum(unpack_rows(d_expert_buf), axis=2))
    d_conv = (d_mid * live_mask * swish_slope(conv_out)).astype(jnp.bfloat16)
    d_conv_f32 = d_conv.astype(jnp.float32)
    d_conv_wide = jnp.pad(d_conv_f32, ((0, 0), (half_taps, half_taps), (0, 0)))
    d_normed = jnp.zeros_like(frames_f32)
    tap_grads = []
    for tap_index in range(TAPS):
        shift_at = 2 * half_taps - tap_index
        d_normed = d_normed + conv_weight[tap_index] * d_conv_wide[:, shift_at:shift_at + LEN]
        tap_grads.append(lax.optimization_barrier(jnp.sum(d_conv_f32 * normed_wide[:, tap_index:tap_index + LEN], axis=(0, 1))))
    d_conv_weight = jnp.stack(tap_grads)
    d_unit = d_normed * live_mask
    d_frames = (d_mid + inv_rms * (d_unit - unit_rows * lax.optimization_barrier(jnp.mean(d_unit * unit_rows, axis=-1, keepdims=True)))).astype(jnp.bfloat16)
    return (block_out, d_frames, d_gate_probs, d_conv_weight, d_weight_in, d_weight_out)
```

```python
import jax
import jax.numpy as jnp
from jax import lax
from jax.sharding import PartitionSpec as P

BF = jnp.bfloat16
F32 = jnp.float32


def swish_slope(value):
    sigmoid_value = jax.nn.sigmoid(value)
    return sigmoid_value + value * sigmoid_value * (1.0 - sigmoid_value)


def cross(value):
    return lax.ppermute(value, "seq", [(s, (s + 4) % 8) for s in range(8)])


def upward(value):
    return lax.ppermute(value, "seq", [(s, s // 4 * 4 + (s + 1) % 4) for s in range(8)])


def downward(value):
    return lax.ppermute(value, "seq", [(s, s // 4 * 4 + (s + 3) % 4) for s in range(8)])


def plane_gather(own0, own1):
    cross0, down0, up0 = cross(own0), upward(own0), downward(own0)
    cross1, down1, up1 = cross(own1), upward(own1), downward(own1)
    cross_down0 = cross(down0)
    far0 = upward(down0)
    cross_up0 = downward(cross0)
    cross_up1 = cross(up1)
    far1 = downward(up1)
    cross_down1 = upward(cross1)
    cross_far0 = upward(cross_down0)
    cross_far1 = downward(cross_up1)
    return (
        [own0, cross0, down0, up0, cross_down0, cross_up0, far0, cross_far0],
        [own1, cross1, down1, up1, cross_down1, cross_up1, far1, cross_far1],
    )


def plus(first, *others):
    total = first.astype(F32)
    for other in others:
        total = total + other.astype(F32)
    return total.astype(BF)


def plane_reduce(half0, half1):
    own0, cross0, down0, up0, cross_down0, cross_up0, far0, cross_far0 = half0
    own1, cross1, down1, up1, cross_down1, cross_up1, far1, cross_far1 = half1
    cross_down0 = plus(cross_down0, downward(cross_far0))
    cross_up1 = plus(cross_up1, upward(cross_far1))
    far0, far1 = downward(far0), upward(far1)
    cross0 = plus(cross0, upward(cross_up0))
    cross1 = plus(cross1, downward(cross_down1))
    up0, down1 = upward(up0), downward(down1)
    down0 = plus(down0, far0, cross(cross_down0))
    up1 = plus(up1, far1, cross(cross_up1))
    own0 = plus(own0, cross(cross0), up0, downward(down0))
    own1 = plus(own1, cross(cross1), down1, upward(up1))
    return own0, own1


def swap_exp(rows):
    return lax.all_to_all(rows, "exp", split_axis=1, concat_axis=1, tiled=True)


def widen_rim(field_in, half_taps):
    count = lax.axis_size("seq")
    ends = count - 1
    frame_count = field_in.shape[0]
    head, tail = field_in[:half_taps], field_in[frame_count - half_taps :]
    return jnp.concatenate(
        [
            lax.ppermute(tail, "seq", [(i, i + 1) for i in range(ends)]),
            field_in,
            lax.ppermute(head, "seq", [(i + 1, i) for i in range(ends)]),
        ],
        axis=0,
    ).astype(F32)


def sum_everywhere(values):
    taps, width = values.shape
    devices = lax.axis_size("seq") * lax.axis_size("exp")
    both = ("seq", "exp")
    rows = -(-taps // 4) * 4
    padded = jnp.pad(values, ((0, rows - taps), (0, 0))).reshape(devices, rows * width // devices)
    mine = jnp.sum(lax.all_to_all(padded, both, split_axis=0, concat_axis=0, tiled=True), axis=0)
    spread = jnp.broadcast_to(mine[None], padded.shape)
    spread = lax.all_to_all(spread, both, split_axis=0, concat_axis=0, tiled=True)
    return spread.reshape(rows, width)[:taps]


def halves(pieces0, pieces1):
    return jnp.stack([jnp.concatenate(pieces0, axis=0), jnp.concatenate(pieces1, axis=0)])


def cut(stage, size):
    return [
        [stage[e, i * size : (i + 1) * size] for i in range(stage.shape[1] // size)] for e in (0, 1)
    ]


def local(
    frames,
    conv_weight,
    gate_probs,
    expert_ids,
    lengths,
    placement,
    weight_in,
    weight_out,
    cotangent,
):
    exp_n = lax.axis_size("exp")
    frame_rows = frames[0]
    frame_count, model_width = frame_rows.shape
    experts = placement.shape[0]
    top_count = expert_ids.shape[2]
    per_dev = weight_in.shape[0]
    capacity = frame_count * top_count // experts
    slots = experts * capacity
    shard = exp_n * capacity
    tap_count = conv_weight.shape[0]
    half_taps = (tap_count - 1) // 2
    positions = lax.axis_index("seq") * frame_count + jnp.arange(frame_count, dtype=jnp.int32)
    live_int = (positions < lengths[0]).astype(jnp.int32)
    live_mask = live_int.astype(F32)[:, None]

    ids_local = expert_ids[0]
    matches = ids_local[:, :, None] == jnp.arange(experts, dtype=jnp.int32)[None, None, :]
    counted = (matches & (live_int == 1)[:, None, None]).astype(F32)
    counted = counted.reshape(frame_count * top_count, experts)
    pair_at = jnp.arange(frame_count * top_count)
    before = (pair_at[:, None] > pair_at[None, :]).astype(BF)
    earlier = jnp.dot(before, counted.astype(BF), preferred_element_type=F32)
    slot_index = jnp.sum(earlier * counted, axis=-1).reshape(frame_count, top_count)
    slot_index = slot_index.astype(jnp.int32)
    kept_bool = (live_int[:, None] == 1) & (slot_index < capacity)
    kept_mask = kept_bool.astype(F32)
    home_slot = jnp.sum(matches.astype(jnp.int32) * placement[None, None, :], axis=-1)
    dest_row = (home_slot % per_dev * exp_n + home_slot // per_dev) * capacity + slot_index
    dest_row = jnp.where(kept_bool, dest_row, -1)
    row_at = jnp.arange(slots, dtype=jnp.int32)
    chosen = dest_row[:, :, None] == row_at
    pick = jnp.any(chosen, axis=1).astype(BF)
    gates_local = gate_probs[0]
    slot_gate = jnp.sum(jnp.where(chosen, gates_local[:, :, None], 0.0), axis=(0, 1))

    def pack(values):
        return jnp.einsum("fs,fd->sd", pick, values, preferred_element_type=F32)

    def unpack(rows):
        by_k = chosen.astype(BF).transpose(1, 0, 2)
        return jnp.einsum("kfs,sd->kfd", by_k, rows, preferred_element_type=F32)

    def to_plane(rows):
        rows = swap_exp(rows.astype(BF).reshape(per_dev, exp_n, capacity, model_width))
        rows = rows.reshape(per_dev, shard, model_width)
        return plane_gather(rows[0], rows[1])

    def from_plane(half0, half1):
        own = jnp.stack(plane_reduce(half0, half1))
        own = swap_exp(own.reshape(per_dev, exp_n, capacity, model_width))
        return own.reshape(slots, model_width)

    cot = cotangent[0]
    grad_pieces = to_plane(pack(cot) * slot_gate[:, None])

    frames_f32 = frame_rows.astype(F32)
    inv_rms = lax.rsqrt(jnp.mean(frames_f32 * frames_f32, axis=-1, keepdims=True) + 1e-06)
    unit_rows = frames_f32 * inv_rms
    normed = (unit_rows * live_mask).astype(BF)
    normed_wide = widen_rim(normed, half_taps)
    conv_out = jnp.zeros_like(frames_f32)
    for tap_index in range(tap_count):
        conv_out = (
            conv_out + normed_wide[tap_index : tap_index + frame_count] * conv_weight[tap_index]
        )
    mid_rows = (frames_f32 + live_mask * jax.nn.silu(conv_out)).astype(BF)
    row_pieces = to_plane(pack(mid_rows))

    def stages(pieces):
        return [halves(pieces[0][:4], pieces[1][:4]), halves(pieces[0][4:], pieces[1][4:])]

    grad_rows = stages(grad_pieces)
    expert_rows = stages(row_pieces)
    out_pieces, in_pieces, d_pres, hiddens = [[], []], [[], []], [], []
    for grads, rows in zip(grad_rows, expert_rows):
        d_hidden = jnp.einsum("erd,efd->erf", grads, weight_out, preferred_element_type=F32)
        pre_act = jnp.einsum("erd,edf->erf", rows, weight_in, preferred_element_type=F32)
        hidden = jax.nn.silu(pre_act).astype(BF)
        d_pre = (d_hidden * swish_slope(pre_act)).astype(BF)
        partial_in = jnp.einsum("erf,edf->erd", d_pre, weight_in, preferred_element_type=F32)
        partial_out = jnp.einsum("erf,efd->erd", hidden, weight_out, preferred_element_type=F32)
        for e in (0, 1):
            in_pieces[e] += cut(partial_in.astype(BF), shard)[e]
            out_pieces[e] += cut(partial_out.astype(BF), shard)[e]
        d_pres.append(d_pre)
        hiddens.append(hidden)

    d_expert_in = unpack(from_plane(*in_pieces))
    expert_out = unpack(from_plane(*out_pieces))

    hidden = jnp.concatenate(hiddens, axis=1)
    d_pre = jnp.concatenate(d_pres, axis=1)
    d_weight_out = jnp.einsum(
        "erf,erd->efd", hidden, jnp.concatenate(grad_rows, axis=1), preferred_element_type=F32
    ).astype(BF)
    d_weight_in = jnp.einsum(
        "erd,erf->edf", jnp.concatenate(expert_rows, axis=1), d_pre, preferred_element_type=F32
    ).astype(BF)

    grad_out = cot.astype(F32)
    gates = (gates_local * kept_mask).T[:, :, None]
    mix_out = jnp.sum(gates * expert_out, axis=0)
    block_out = (mid_rows.astype(F32) + mix_out).astype(BF)
    d_gate_probs = kept_mask * jnp.sum(grad_out[None] * expert_out, axis=-1).T

    d_mid = grad_out + jnp.sum(d_expert_in, axis=0)
    d_conv = (d_mid * live_mask * swish_slope(conv_out)).astype(BF)
    d_conv_f32 = d_conv.astype(F32)
    d_conv_wide = widen_rim(d_conv, half_taps)
    d_normed = jnp.zeros_like(frames_f32)
    tap_grads = []
    for tap_index in range(tap_count):
        shift_at = 2 * half_taps - tap_index
        d_normed = (
            d_normed + conv_weight[tap_index] * d_conv_wide[shift_at : shift_at + frame_count]
        )
        tap_grads.append(
            jnp.sum(d_conv_f32 * normed_wide[tap_index : tap_index + frame_count], axis=0)
        )
    d_conv_weight = sum_everywhere(jnp.stack(tap_grads))
    d_unit = d_normed * live_mask
    d_frames = (
        d_mid
        + inv_rms * (d_unit - unit_rows * jnp.mean(d_unit * unit_rows, axis=-1, keepdims=True))
    ).astype(BF)
    return (
        block_out[None],
        d_frames[None],
        d_gate_probs[None],
        d_conv_weight,
        d_weight_in,
        d_weight_out,
    )


def solution(mesh):
    in_specs = (
        P("exp", "seq", None),
        P(),
        P("exp", "seq", None),
        P("exp", "seq", None),
        P("exp"),
        P(),
        P("exp", None, "seq"),
        P("exp", "seq", None),
        P("exp", "seq", None),
    )
    out_specs = (
        P("exp", "seq", None),
        P("exp", "seq", None),
        P("exp", "seq", None),
        P(),
        P("exp", None, "seq"),
        P("exp", "seq", None),
    )
    return jax.shard_map(local, mesh=mesh, in_specs=in_specs, out_specs=out_specs, check_vma=False)
```

```python
import functools

import jax
import jax.numpy as jnp
from jax import lax
from jax.experimental import pallas as pl
from jax.experimental.pallas import tpu as pltpu
from jax.sharding import PartitionSpec as P

BF = jnp.bfloat16
F32 = jnp.float32


def swish_slope(value):
    sigmoid_value = jax.nn.sigmoid(value)
    return sigmoid_value + value * sigmoid_value * (1.0 - sigmoid_value)


def cross(value):
    return lax.ppermute(value, "seq", [(s, (s + 4) % 8) for s in range(8)])


def upward(value):
    return lax.ppermute(value, "seq", [(s, s // 4 * 4 + (s + 1) % 4) for s in range(8)])


def downward(value):
    return lax.ppermute(value, "seq", [(s, s // 4 * 4 + (s + 3) % 4) for s in range(8)])


def tied(values, *others):
    return lax.optimization_barrier((values, others))[0]


def gather_first(own):
    return own, cross(own), upward(own), downward(own)


def gather_second_sends(first):
    _, over, down, up = first
    return (
        jnp.stack([down[0], up[1]]),
        jnp.stack([down[0], over[1]]),
        jnp.stack([over[0], up[1]]),
    )


def gather_second(sends):
    return cross(sends[0]), upward(sends[1]), downward(sends[2])


def gather_third(over2):
    return (jnp.stack([upward(over2[0]), downward(over2[1])]),)


def plus(*terms):
    return sum(term.astype(F32) for term in terms).astype(BF)


def reduce_first(third):
    return downward(third[0]), upward(third[1])


def reduce_second(second, far):
    over2, down2, up2 = second
    over2 = cross(jnp.stack([plus(over2[0], far[0]), plus(over2[1], far[1])]))
    return over2, downward(down2), upward(up2)


def reduce_third(first, second):
    own, over, down, up = first
    over2, down2, up2 = second
    down = jnp.stack([plus(down[0], over2[0], down2[0]), down[1]])
    up = jnp.stack([up[0], plus(up[1], over2[1], up2[1])])
    over = jnp.stack([plus(over[0], up2[0]), plus(over[1], down2[1])])
    return own, over, down, up


def reduce_end(own, over, down, up):
    return plus(own, cross(over), downward(down), upward(up))


def swap_exp(rows):
    return lax.all_to_all(rows, "exp", split_axis=1, concat_axis=1, tiled=True)


def widen_rim(field_in, half_taps):
    count = lax.axis_size("seq")
    ends = count - 1
    frame_count = field_in.shape[0]
    head, tail = field_in[:half_taps], field_in[frame_count - half_taps :]
    return jnp.concatenate(
        [
            lax.ppermute(tail, "seq", [(i, i + 1) for i in range(ends)]),
            field_in,
            lax.ppermute(head, "seq", [(i + 1, i) for i in range(ends)]),
        ],
        axis=0,
    ).astype(F32)


def sum_everywhere(values):
    both = ("seq", "exp")
    mine = jnp.sum(lax.all_to_all(values, both, split_axis=0, concat_axis=0, tiled=True), axis=0)
    spread = jnp.broadcast_to(mine[None], values.shape)
    return lax.all_to_all(spread, both, split_axis=0, concat_axis=0, tiled=True)


NT = (((1,), (1,)), ((), ()))


def cost(flops):
    return pl.CostEstimate(flops=flops // 3, bytes_accessed=1 << 20, transcendentals=0)


def join(pieces, whole):
    shard = pieces[0].shape[1]
    for i, piece in enumerate(pieces):
        whole[i * shard : (i + 1) * shard] = piece[0]


def part_of(whole, pieces):
    shard = pieces[0].shape[1]
    for i, piece in enumerate(pieces):
        piece[0] = whole[i * shard : (i + 1) * shard].astype(BF)


def d_hidden_kernel(count, *refs):
    grads, (weight_out, d_hidden, whole) = refs[:count], refs[count:]

    @pl.when(pl.program_id(1) == 0)
    def _():
        join(grads, whole)

    d_hidden[0] = lax.dot_general(whole[...], weight_out[0], NT, preferred_element_type=F32)


def hidden_kernel(count, group, *refs):
    rows, (weight_in, d_hidden) = refs[:count], refs[count : count + 2]
    lot, (hidden_ref, d_pre_ref) = refs[count + 2 : 2 * count + 2], refs[2 * count + 2 :]
    shard = rows[0].shape[1]
    weights = weight_in[0]
    for first in range(0, count, group):
        mine = range(first, min(first + group, count))
        at = slice(first * shard, (mine[-1] + 1) * shard)
        block = jnp.concatenate([rows[i][0] for i in mine], axis=0)
        pre_act = jnp.dot(block, weights, preferred_element_type=F32)
        gate = jax.nn.sigmoid(pre_act)
        swish = pre_act * gate
        d_pre = (d_hidden[0, at] * (gate + swish * (1.0 - gate))).astype(BF)
        hidden_ref[0, at] = swish.astype(BF)
        d_pre_ref[0, at] = d_pre
        back = lax.dot_general(d_pre, weights, NT, preferred_element_type=F32).astype(BF)
        for i in mine:
            lot[i][0] = back[(i - first) * shard : (i - first + 1) * shard]


def out_kernel(count, *refs):
    hidden, weight_out = refs[:2]
    lot, total = refs[2:-1], refs[-1]
    total[...] = jnp.dot(hidden[0], weight_out[0], preferred_element_type=F32)
    part_of(total, lot)


TN = (((0,), (0,)), ((), ()))


def grad_in_kernel(count, *refs):
    rows, d_pres, (out,) = refs[:count], refs[count:-1], refs[-1:]
    left = jnp.concatenate([row[0] for row in rows], axis=0)
    right = jnp.concatenate([d_pre[0] for d_pre in d_pres], axis=0)
    out[0] = lax.dot_general(left, right, TN, preferred_element_type=F32).astype(BF)


def grad_out_kernel(count, *refs):
    grads, hiddens, (out,) = refs[:count], refs[count:-1], refs[-1:]
    left = jnp.concatenate([hidden[0] for hidden in hiddens], axis=0)
    right = jnp.concatenate([grad[0] for grad in grads], axis=0)
    out[0] = lax.dot_general(left, right, TN, preferred_element_type=F32).astype(BF)


def grad_in_of(rows, d_pres):
    count = len(rows)
    per_dev, shard, width = rows[0].shape
    units = d_pres[0].shape[2]
    return pl.pallas_call(
        functools.partial(grad_in_kernel, count),
        grid=(per_dev, width // BLOCK),
        in_specs=[pl.BlockSpec((1, shard, BLOCK), lambda e, d: (e, 0, d))] * count
        + [pl.BlockSpec((1, d_pre.shape[1], units), lambda e, d: (e, 0, 0)) for d_pre in d_pres],
        out_specs=pl.BlockSpec((1, BLOCK, units), lambda e, d: (e, d, 0)),
        out_shape=jax.ShapeDtypeStruct((per_dev, width, units), BF),
        compiler_params=LIMIT,
        cost_estimate=cost(2 * per_dev * count * shard * units * width),
        name="grad_in",
    )(*rows, *d_pres)


def grad_out_of(grads, hiddens):
    count = len(grads)
    per_dev, shard, width = grads[0].shape
    units = hiddens[0].shape[2]
    return pl.pallas_call(
        functools.partial(grad_out_kernel, count),
        grid=(per_dev, units // BLOCK),
        in_specs=[piece_spec(shard, width)] * count
        + [
            pl.BlockSpec((1, hidden.shape[1], BLOCK), lambda e, f: (e, 0, f)) for hidden in hiddens
        ],
        out_specs=pl.BlockSpec((1, BLOCK, width), lambda e, f: (e, f, 0)),
        out_shape=jax.ShapeDtypeStruct((per_dev, units, width), BF),
        compiler_params=LIMIT,
        cost_estimate=cost(2 * per_dev * count * shard * units * width),
        name="grad_out",
    )(*grads, *hiddens)


def conv_back_kernel(taps, pick, rows, cot, slope, wide, d_mid_ref, d_conv_ref, tap_ref):
    frame_count = cot.shape[0]
    d_mid = cot[...].astype(F32) + jnp.dot(pick[...], rows[...], preferred_element_type=F32)
    d_conv = (d_mid * slope[...]).astype(BF)
    d_mid_ref[...] = d_mid
    d_conv_ref[...] = d_conv
    d_conv = d_conv.astype(F32)
    tap_ref[...] = jnp.zeros_like(tap_ref)
    for tap in range(taps):
        product = d_conv * wide[tap : tap + frame_count]
        tap_ref[tap : tap + 1] = jnp.sum(product, axis=0, keepdims=True)


def conv_back_of(pick, rows, cot, slope, wide, taps):
    frame_count, width = cot.shape
    block, held = width // 4, -(-taps // 8) * 8

    def columns(array):
        return pl.BlockSpec((array.shape[0], block), lambda c: (0, c))

    return pl.pallas_call(
        functools.partial(conv_back_kernel, taps),
        grid=(4,),
        in_specs=[pl.BlockSpec(pick.shape, lambda c: (0, 0))]
        + [columns(array) for array in (rows, cot, slope, wide)],
        out_specs=[columns(cot), columns(cot), pl.BlockSpec((held, block), lambda c: (c, 0))],
        out_shape=[
            jax.ShapeDtypeStruct((frame_count, width), F32),
            jax.ShapeDtypeStruct((frame_count, width), BF),
            jax.ShapeDtypeStruct((4 * held, block), F32),
        ],
        compiler_params=LIMIT,
        cost_estimate=pl.CostEstimate(flops=1 << 20, bytes_accessed=1 << 22, transcendentals=0),
        name="conv_back",
    )(pick, rows, cot, slope, wide)


BLOCK = 256
LIMIT = pltpu.CompilerParams(vmem_limit_bytes=40 << 20)


def piece_spec(shard, width):
    return pl.BlockSpec((1, shard, width), lambda e, f: (e, 0, 0))


def d_hidden_of(grads, weight_out):
    count = len(grads)
    per_dev, shard, width = grads[0].shape
    units, total = weight_out.shape[1], count * shard
    return pl.pallas_call(
        functools.partial(d_hidden_kernel, count),
        grid=(per_dev, units // BLOCK),
        in_specs=[piece_spec(shard, width)] * count
        + [pl.BlockSpec((1, BLOCK, width), lambda e, f: (e, f, 0))],
        out_specs=pl.BlockSpec((1, total, BLOCK), lambda e, f: (e, 0, f)),
        out_shape=jax.ShapeDtypeStruct((per_dev, total, units), F32),
        scratch_shapes=[pltpu.VMEM((total, width), BF)],
        compiler_params=LIMIT,
        cost_estimate=cost(2 * per_dev * total * units * width),
        name="d_hidden",
    )(*grads, weight_out)


def hidden_of(rows, weight_in, d_hidden):
    count = len(rows)
    per_dev, shard, width = rows[0].shape
    units, total = weight_in.shape[2], count * shard
    inner = pl.BlockSpec((1, total, units), lambda e: (e, 0, 0))
    inner_shape = jax.ShapeDtypeStruct((per_dev, total, units), BF)
    piece = pl.BlockSpec((1, shard, width), lambda e: (e, 0, 0))
    outs = pl.pallas_call(
        functools.partial(hidden_kernel, count, 2),
        grid=(per_dev,),
        in_specs=[piece] * count
        + [pl.BlockSpec((1, width, units), lambda e: (e, 0, 0)), inner],
        out_specs=[piece] * count + [inner] * 2,
        out_shape=[jax.ShapeDtypeStruct((per_dev, shard, width), BF)] * count + [inner_shape] * 2,
        compiler_params=LIMIT,
        cost_estimate=cost(4 * per_dev * total * units * width),
        name="hidden",
    )(*rows, weight_in, d_hidden)
    return outs[:count], outs[count], outs[count + 1]


def out_of(hidden, weight_out, shard):
    per_dev, total, units = hidden.shape
    width = weight_out.shape[2]
    count = total // shard
    piece = pl.BlockSpec((1, shard, width), lambda e: (e, 0, 0))
    return pl.pallas_call(
        functools.partial(out_kernel, count),
        grid=(per_dev,),
        in_specs=[
            pl.BlockSpec((1, total, units), lambda e: (e, 0, 0)),
            pl.BlockSpec((1, units, width), lambda e: (e, 0, 0)),
        ],
        out_specs=[piece] * count,
        out_shape=[jax.ShapeDtypeStruct((per_dev, shard, width), BF)] * count,
        scratch_shapes=[pltpu.VMEM((total, width), F32)],
        compiler_params=LIMIT,
        cost_estimate=cost(2 * per_dev * total * units * width),
        name="partial_out",
    )(hidden, weight_out)


def local(
    frames,
    conv_weight,
    gate_probs,
    expert_ids,
    lengths,
    placement,
    weight_in,
    weight_out,
    cotangent,
):
    exp_n = lax.axis_size("exp")
    frame_rows = frames[0]
    frame_count, model_width = frame_rows.shape
    experts = placement.shape[0]
    top_count = expert_ids.shape[2]
    per_dev = weight_in.shape[0]
    capacity = frame_count * top_count // experts
    slots = experts * capacity
    shard = exp_n * capacity
    tap_count = conv_weight.shape[0]
    half_taps = (tap_count - 1) // 2
    positions = lax.axis_index("seq") * frame_count + jnp.arange(frame_count, dtype=jnp.int32)
    live_int = (positions < lengths[0]).astype(jnp.int32)
    live_mask = live_int.astype(F32)[:, None]

    ids_local = expert_ids[0]
    matches = ids_local[:, :, None] == jnp.arange(experts, dtype=jnp.int32)[None, None, :]
    counted = (matches & (live_int == 1)[:, None, None]).astype(F32)
    counted = counted.reshape(frame_count * top_count, experts)
    pair_at = jnp.arange(frame_count * top_count)
    before = (pair_at[:, None] > pair_at[None, :]).astype(BF)
    earlier = jnp.dot(before, counted.astype(BF), preferred_element_type=F32)
    slot_index = jnp.sum(earlier * counted, axis=-1).reshape(frame_count, top_count)
    slot_index = slot_index.astype(jnp.int32)
    kept_bool = (live_int[:, None] == 1) & (slot_index < capacity)
    kept_mask = kept_bool.astype(F32)
    home_slot = jnp.sum(matches.astype(jnp.int32) * placement[None, None, :], axis=-1)
    dest_row = (home_slot % per_dev * exp_n + home_slot // per_dev) * capacity + slot_index
    dest_row = jnp.where(kept_bool, dest_row, -1)
    row_at = jnp.arange(slots, dtype=jnp.int32)
    chosen = dest_row[:, :, None] == row_at
    pick = jnp.any(chosen, axis=1).astype(BF)
    gates_local = gate_probs[0]
    slot_gate = jnp.sum(jnp.where(chosen, gates_local[:, :, None], 0.0), axis=(0, 1))

    def pack(values):
        return jnp.einsum("fs,fd->sd", pick, values, preferred_element_type=F32)

    def unpack(rows):
        by_k = chosen.astype(BF).transpose(1, 0, 2)
        return jnp.einsum("kfs,sd->kfd", by_k, rows, preferred_element_type=F32)

    def to_plane(rows):
        rows = swap_exp(rows.reshape(per_dev, exp_n, capacity, model_width))
        return rows.reshape(per_dev, shard, model_width)

    def from_plane(own):
        own = swap_exp(own.reshape(per_dev, exp_n, capacity, model_width))
        return own.reshape(slots, model_width)

    cot = cotangent[0]
    packed_grads = (pack(cot) * slot_gate[:, None]).astype(BF)
    own_grads = to_plane(packed_grads)

    frames_f32 = frame_rows.astype(F32)
    inv_rms = lax.rsqrt(jnp.mean(frames_f32 * frames_f32, axis=-1, keepdims=True) + 1e-06)
    unit_rows = frames_f32 * inv_rms
    normed = (unit_rows * live_mask).astype(BF)
    normed = tied(normed, packed_grads)
    normed_wide = widen_rim(normed, half_taps)
    conv_out = jnp.zeros_like(frames_f32)
    for tap_index in range(tap_count):
        conv_out = (
            conv_out + normed_wide[tap_index : tap_index + frame_count] * conv_weight[tap_index]
        )
    mid_rows = (frames_f32 + live_mask * jax.nn.silu(conv_out)).astype(BF)
    packed_rows = pack(mid_rows).astype(BF)

    grad1 = gather_first(own_grads)
    own_rows = to_plane(tied(packed_rows, grad1))
    grad2 = gather_second(gather_second_sends(grad1))
    d_hidden1 = d_hidden_of(grad1, weight_out)
    own_rows, over2 = tied((own_rows, grad2[0]), d_hidden1)
    row1 = gather_first(own_rows)
    grad3 = gather_third(over2)
    d_hidden2 = d_hidden_of(grad2, weight_out)
    row2 = gather_second(tied(gather_second_sends(row1), d_hidden2, grad3))
    d_hidden3 = d_hidden_of(grad3, weight_out)
    lot1, hidden1, d_pre1 = hidden_of(row1, weight_in, d_hidden1)
    row3 = gather_third(tied(row2[0], d_hidden3, d_pre1))
    lot2, hidden2, d_pre2 = hidden_of(row2, weight_in, d_hidden2)
    lot3, hidden3, d_pre3 = hidden_of(tied(row3, d_pre2), weight_in, d_hidden3)
    hiddens, d_pres = (hidden1, hidden2, hidden3), (d_pre1, d_pre2, d_pre3)

    in1 = reduce_first(lot3[0])
    outs = [out_of(hidden, weight_out, shard) for hidden in tied(hiddens, lot3)]
    lot1, lot2, in1, d_pres, out_lot3 = tied((lot1, lot2, in1, d_pres, outs[2][0]), outs)
    in2 = reduce_second(lot2, in1)
    out1 = reduce_first(out_lot3)
    d_weight_in = grad_in_of((*row1, *row2, *row3), d_pres)
    lot1, in2, hiddens, out1, outs = tied((lot1, in2, hiddens, out1, outs), d_weight_in)
    in3 = reduce_third(lot1, in2)
    outs, out1 = tied((outs, out1), in3)
    own_in = reduce_end(*in3)
    out2 = reduce_second(outs[1], out1)
    d_weight_out = grad_out_of((*grad1, *grad2, *grad3), hiddens)
    own_in = tied(own_in, d_weight_out)
    rows_in = from_plane(own_in)
    out3 = reduce_third(outs[0], out2)
    own_out = reduce_end(*out3)
    expert_out = unpack(from_plane(own_out))

    grad_out = cot.astype(F32)
    gates = (gates_local * kept_mask).T[:, :, None]
    mix_out = jnp.sum(gates * expert_out, axis=0)
    block_out = (mid_rows.astype(F32) + mix_out).astype(BF)
    d_gate_probs = kept_mask * jnp.sum(grad_out[None] * expert_out, axis=-1).T

    slope = live_mask * swish_slope(conv_out)
    d_mid, d_conv, tap_grads = conv_back_of(pick, rows_in, cot, slope, normed_wide, tap_count)
    d_conv_wide = widen_rim(d_conv, half_taps)
    d_normed = jnp.zeros_like(frames_f32)
    for tap_index in range(tap_count):
        shift_at = 2 * half_taps - tap_index
        d_normed = (
            d_normed + conv_weight[tap_index] * d_conv_wide[shift_at : shift_at + frame_count]
        )
    tap_sums = sum_everywhere(tied(tap_grads, out3)).reshape(4, -1, model_width // 4)
    d_conv_weight = tap_sums.transpose(1, 0, 2).reshape(-1, model_width)[:tap_count]
    d_unit = d_normed * live_mask
    d_frames = (
        d_mid
        + inv_rms * (d_unit - unit_rows * jnp.mean(d_unit * unit_rows, axis=-1, keepdims=True))
    ).astype(BF)
    return (
        block_out[None],
        d_frames[None],
        d_gate_probs[None],
        d_conv_weight,
        d_weight_in,
        d_weight_out,
    )


def solution(mesh):
    in_specs = (
        P("exp", "seq", None),
        P(),
        P("exp", "seq", None),
        P("exp", "seq", None),
        P("exp"),
        P(),
        P("exp", None, "seq"),
        P("exp", "seq", None),
        P("exp", "seq", None),
    )
    out_specs = (
        P("exp", "seq", None),
        P("exp", "seq", None),
        P("exp", "seq", None),
        P(),
        P("exp", None, "seq"),
        P("exp", "seq", None),
    )
    return jax.shard_map(local, mesh=mesh, in_specs=in_specs, out_specs=out_specs, check_vma=False)
```

```python
import functools

import jax
import jax.numpy as jnp
from jax import lax
from jax.experimental import pallas as pl
from jax.experimental.pallas import tpu as pltpu
from jax.sharding import PartitionSpec as P

BF = jnp.bfloat16
F32 = jnp.float32


def swish_slope(value):
    sigmoid_value = jax.nn.sigmoid(value)
    return sigmoid_value + value * sigmoid_value * (1.0 - sigmoid_value)


def cross(value):
    return lax.ppermute(value, "seq", [(s, (s + 4) % 8) for s in range(8)])


def upward(value):
    return lax.ppermute(value, "seq", [(s, s // 4 * 4 + (s + 1) % 4) for s in range(8)])


def downward(value):
    return lax.ppermute(value, "seq", [(s, s // 4 * 4 + (s + 3) % 4) for s in range(8)])


def tied(values, *others):
    return lax.optimization_barrier((values, others))[0]


def gather_first(own):
    return own, cross(own), upward(own), downward(own)


def gather_second_sends(first):
    _, over, down, up = first
    return (
        jnp.stack([down[0], up[1]]),
        jnp.stack([down[0], over[1]]),
        jnp.stack([over[0], up[1]]),
    )


def gather_second(sends):
    return cross(sends[0]), upward(sends[1]), downward(sends[2])


def gather_third(sends):
    return upward(sends[0]), downward(sends[1])


def plus(*terms):
    return sum(term.astype(F32) for term in terms).astype(BF)


def reduce_first(third):
    return downward(third[0]), upward(third[1])


def reduce_second_over(second, far):
    return jnp.stack([plus(second[0][0], far[0]), plus(second[0][1], far[1])])


def reduce_second_along(second):
    return downward(second[1]), upward(second[2])


def reduce_third(first, second):
    own, over, down, up = first
    over2, down2, up2 = second
    down = jnp.stack([plus(down[0], over2[0], down2[0]), down[1]])
    up = jnp.stack([up[0], plus(up[1], over2[1], up2[1])])
    over = jnp.stack([plus(over[0], up2[0]), plus(over[1], down2[1])])
    return own, over, down, up


def reduce_end(own, over, down, up):
    return plus(own, cross(over), downward(down), upward(up))


def swap_exp(rows):
    return lax.all_to_all(rows, "exp", split_axis=0, concat_axis=0, tiled=True)


def widen_rim(field_in, half_taps):
    count = lax.axis_size("seq")
    ends = count - 1
    frame_count = field_in.shape[0]
    head, tail = field_in[:half_taps], field_in[frame_count - half_taps :]
    return jnp.concatenate(
        [
            lax.ppermute(tail, "seq", [(i, i + 1) for i in range(ends)]),
            field_in,
            lax.ppermute(head, "seq", [(i + 1, i) for i in range(ends)]),
        ],
        axis=0,
    ).astype(F32)


def send(value, axis, step):
    def target(at):
        seq, exp = divmod(at, 16)
        low, y, high, z, core = seq // 4, seq % 4, exp // 8, exp // 2 % 4, exp % 2
        x = high * 2 + low
        if axis == "x":
            x = (x + step) % 4
        elif axis == "y":
            y = (y + step) % 4
        elif axis == "z":
            z = (z + step) % 4
        else:
            core = 1 - core
        return ((x % 2) * 4 + y) * 16 + (x // 2) * 8 + z * 2 + core

    return lax.ppermute(value, ("seq", "exp"), [(at, target(at)) for at in range(128)])


def sum_everywhere(values, others):
    count = values.shape[0] // 2
    first = lax.axis_index("exp") % 2 == 0
    low, high = values[:count], values[count:]
    half = jnp.where(first, low, high) + send(jnp.where(first, high, low), "core", 1)
    for axis, before in (("z", others), ("y", ()), ("x", ())):
        half = tied(half, before)
        half = (half + send(half, axis, 2)) + (send(half, axis, 1) + send(half, axis, 3))
    other = send(half, "core", 1)
    return jnp.concatenate([jnp.where(first, half, other), jnp.where(first, other, half)])


NT = (((1,), (1,)), ((), ()))


def cost(flops):
    return pl.CostEstimate(flops=flops // 4096, bytes_accessed=1 << 10, transcendentals=0)


def join(pieces, whole):
    shard = pieces[0].shape[1]
    for i, piece in enumerate(pieces):
        whole[i * shard : (i + 1) * shard] = piece[0]


def part_of(whole, pieces):
    shard = pieces[0].shape[1]
    for i, piece in enumerate(pieces):
        piece[0] = whole[i * shard : (i + 1) * shard].astype(BF)


def d_hidden_kernel(count, *refs):
    grads, (weight_out, d_hidden, whole) = refs[:count], refs[count:]

    @pl.when(pl.program_id(1) == 0)
    def _():
        join(grads, whole)

    d_hidden[0] = lax.dot_general(whole[...], weight_out[0], NT, preferred_element_type=F32)


def hidden_kernel(count, group, *refs):
    rows, (weight_in, d_hidden) = refs[:count], refs[count : count + 2]
    lot, (hidden_ref, d_pre_ref) = refs[count + 2 : 2 * count + 2], refs[2 * count + 2 :]
    shard = rows[0].shape[1]
    weights = weight_in[0]
    for first in range(0, count, group):
        mine = range(first, min(first + group, count))
        at = slice(first * shard, (mine[-1] + 1) * shard)
        block = jnp.concatenate([rows[i][0] for i in mine], axis=0)
        pre_act = jnp.dot(block, weights, preferred_element_type=F32)
        gate = jax.nn.sigmoid(pre_act)
        swish = pre_act * gate
        d_pre = (d_hidden[0, at] * (gate + swish * (1.0 - gate))).astype(BF)
        hidden_ref[0, at] = swish.astype(BF)
        d_pre_ref[0, at] = d_pre
        back = lax.dot_general(d_pre, weights, NT, preferred_element_type=F32).astype(BF)
        for i in mine:
            lot[i][0] = back[(i - first) * shard : (i - first + 1) * shard]


def out_kernel(count, *refs):
    hidden, weight_out = refs[:2]
    lot, total = refs[2:-1], refs[-1]
    total[...] = jnp.dot(hidden[0], weight_out[0], preferred_element_type=F32)
    part_of(total, lot)


TN = (((0,), (0,)), ((), ()))


def grad_in_kernel(count, *refs):
    rows, d_pres, (out,) = refs[:count], refs[count:-1], refs[-1:]
    left = jnp.concatenate([row[0] for row in rows], axis=0)
    right = jnp.concatenate([d_pre[0] for d_pre in d_pres], axis=0)
    out[0] = lax.dot_general(left, right, TN, preferred_element_type=F32).astype(BF)


def grad_out_kernel(count, *refs):
    grads, hiddens, (out,) = refs[:count], refs[count:-1], refs[-1:]
    left = jnp.concatenate([hidden[0] for hidden in hiddens], axis=0)
    right = jnp.concatenate([grad[0] for grad in grads], axis=0)
    out[0] = lax.dot_general(left, right, TN, preferred_element_type=F32).astype(BF)


def grad_in_of(rows, d_pres):
    count = len(rows)
    per_dev, shard, width = rows[0].shape
    units = d_pres[0].shape[2]
    return pl.pallas_call(
        functools.partial(grad_in_kernel, count),
        grid=(per_dev, width // BLOCK),
        in_specs=[pl.BlockSpec((1, shard, BLOCK), lambda e, d: (e, 0, d))] * count
        + [pl.BlockSpec((1, d_pre.shape[1], units), lambda e, d: (e, 0, 0)) for d_pre in d_pres],
        out_specs=pl.BlockSpec((1, BLOCK, units), lambda e, d: (e, d, 0)),
        out_shape=jax.ShapeDtypeStruct((per_dev, width, units), BF),
        compiler_params=LIMIT,
        cost_estimate=cost(2 * per_dev * count * shard * units * width),
        name="grad_in",
    )(*rows, *d_pres)


def grad_out_of(grads, hiddens):
    count = len(grads)
    per_dev, shard, width = grads[0].shape
    units = hiddens[0].shape[2]
    return pl.pallas_call(
        functools.partial(grad_out_kernel, count),
        grid=(per_dev, units // BLOCK),
        in_specs=[piece_spec(shard, width)] * count
        + [
            pl.BlockSpec((1, hidden.shape[1], BLOCK), lambda e, f: (e, 0, f)) for hidden in hiddens
        ],
        out_specs=pl.BlockSpec((1, BLOCK, width), lambda e, f: (e, f, 0)),
        out_shape=jax.ShapeDtypeStruct((per_dev, units, width), BF),
        compiler_params=LIMIT,
        cost_estimate=cost(2 * per_dev * count * shard * units * width),
        name="grad_out",
    )(*grads, *hiddens)


def conv_back_kernel(taps, pick, rows, cot, slope, wide, d_mid_ref, d_conv_ref, tap_ref):
    frame_count = cot.shape[0]
    d_mid = cot[...].astype(F32) + jnp.dot(pick[...], rows[...], preferred_element_type=F32)
    d_conv = (d_mid * slope[...]).astype(BF)
    d_mid_ref[...] = d_mid
    d_conv_ref[...] = d_conv
    d_conv = d_conv.astype(F32)
    tap_ref[...] = jnp.zeros_like(tap_ref)
    for tap in range(taps):
        product = d_conv * wide[tap : tap + frame_count]
        tap_ref[tap : tap + 1] = jnp.sum(product, axis=0, keepdims=True)


def conv_back_of(pick, rows, cot, slope, wide, taps):
    frame_count, width = cot.shape
    block, held = width // 4, -(-taps // 8) * 8

    def columns(array):
        return pl.BlockSpec((array.shape[0], block), lambda c: (0, c))

    return pl.pallas_call(
        functools.partial(conv_back_kernel, taps),
        grid=(4,),
        in_specs=[pl.BlockSpec(pick.shape, lambda c: (0, 0))]
        + [columns(array) for array in (rows, cot, slope, wide)],
        out_specs=[columns(cot), columns(cot), pl.BlockSpec((held, block), lambda c: (c, 0))],
        out_shape=[
            jax.ShapeDtypeStruct((frame_count, width), F32),
            jax.ShapeDtypeStruct((frame_count, width), BF),
            jax.ShapeDtypeStruct((4 * held, block), F32),
        ],
        compiler_params=LIMIT,
        cost_estimate=pl.CostEstimate(flops=1 << 20, bytes_accessed=1 << 22, transcendentals=0),
        name="conv_back",
    )(pick, rows, cot, slope, wide)


BLOCK = 256
LIMIT = pltpu.CompilerParams(vmem_limit_bytes=24 << 20)


def piece_spec(shard, width):
    return pl.BlockSpec((1, shard, width), lambda e, f: (e, 0, 0))


def d_hidden_of(grads, weight_out):
    count = len(grads)
    per_dev, shard, width = grads[0].shape
    units, total = weight_out.shape[1], count * shard
    return pl.pallas_call(
        functools.partial(d_hidden_kernel, count),
        grid=(per_dev, units // BLOCK),
        in_specs=[piece_spec(shard, width)] * count
        + [pl.BlockSpec((1, BLOCK, width), lambda e, f: (e, f, 0))],
        out_specs=pl.BlockSpec((1, total, BLOCK), lambda e, f: (e, 0, f)),
        out_shape=jax.ShapeDtypeStruct((per_dev, total, units), F32),
        scratch_shapes=[pltpu.VMEM((total, width), BF)],
        compiler_params=LIMIT,
        cost_estimate=cost(2 * per_dev * total * units * width),
        name="d_hidden",
    )(*grads, weight_out)


def hidden_of(rows, weight_in, d_hidden):
    count = len(rows)
    per_dev, shard, width = rows[0].shape
    units, total = weight_in.shape[2], count * shard
    inner = pl.BlockSpec((1, total, units), lambda e: (e, 0, 0))
    inner_shape = jax.ShapeDtypeStruct((per_dev, total, units), BF)
    piece = pl.BlockSpec((1, shard, width), lambda e: (e, 0, 0))
    outs = pl.pallas_call(
        functools.partial(hidden_kernel, count, 2),
        grid=(per_dev,),
        in_specs=[piece] * count
        + [pl.BlockSpec((1, width, units), lambda e: (e, 0, 0)), inner],
        out_specs=[piece] * count + [inner] * 2,
        out_shape=[jax.ShapeDtypeStruct((per_dev, shard, width), BF)] * count + [inner_shape] * 2,
        compiler_params=LIMIT,
        cost_estimate=cost(4 * per_dev * total * units * width),
        name="hidden",
    )(*rows, weight_in, d_hidden)
    return outs[:count], outs[count], outs[count + 1]


def far_kernel(grads0, grads1, rows0, rows1, weight_in, weight_out, lot, hidden_ref, d_pre_ref):
    first = pl.program_id(0) == 0
    grads = jnp.where(first, grads0[...], grads1[...])
    rows = jnp.where(first, rows0[...], rows1[...])
    d_hidden = lax.dot_general(grads, weight_out[0], NT, preferred_element_type=F32)
    pre_act = jnp.dot(rows, weight_in[0], preferred_element_type=F32)
    gate = jax.nn.sigmoid(pre_act)
    swish = pre_act * gate
    d_pre = (d_hidden * (gate + swish * (1.0 - gate))).astype(BF)
    hidden_ref[0] = swish.astype(BF)
    d_pre_ref[0] = d_pre
    lot[0] = lax.dot_general(d_pre, weight_in[0], NT, preferred_element_type=F32).astype(BF)


def far_of(grads, rows, weight_in, weight_out):
    shard, width = rows[0].shape
    per_dev, units = weight_out.shape[:2]

    def whole(rows_n, columns):
        return pl.BlockSpec((1, rows_n, columns), lambda e: (e, 0, 0))

    return pl.pallas_call(
        far_kernel,
        grid=(per_dev,),
        in_specs=[pl.BlockSpec((shard, width), lambda e: (0, 0))] * 4
        + [whole(width, units), whole(units, width)],
        out_specs=[whole(shard, width)] + [whole(shard, units)] * 2,
        out_shape=[jax.ShapeDtypeStruct((per_dev, shard, width), BF)]
        + [jax.ShapeDtypeStruct((per_dev, shard, units), BF)] * 2,
        compiler_params=LIMIT,
        cost_estimate=cost(6 * per_dev * shard * units * width),
        name="far",
    )(*grads, *rows, weight_in, weight_out)


def out_of(hidden, weight_out, shard):
    per_dev, total, units = hidden.shape
    width = weight_out.shape[2]
    count = total // shard
    piece = pl.BlockSpec((1, shard, width), lambda e: (e, 0, 0))
    return pl.pallas_call(
        functools.partial(out_kernel, count),
        grid=(per_dev,),
        in_specs=[
            pl.BlockSpec((1, total, units), lambda e: (e, 0, 0)),
            pl.BlockSpec((1, units, width), lambda e: (e, 0, 0)),
        ],
        out_specs=[piece] * count,
        out_shape=[jax.ShapeDtypeStruct((per_dev, shard, width), BF)] * count,
        scratch_shapes=[pltpu.VMEM((total, width), F32)],
        compiler_params=LIMIT,
        cost_estimate=cost(2 * per_dev * total * units * width),
        name="partial_out",
    )(hidden, weight_out)


def local(
    frames,
    conv_weight,
    gate_probs,
    expert_ids,
    lengths,
    placement,
    weight_in,
    weight_out,
    cotangent,
):
    exp_n = lax.axis_size("exp")
    frame_rows = frames[0]
    frame_count, model_width = frame_rows.shape
    experts = placement.shape[0]
    top_count = expert_ids.shape[2]
    per_dev = weight_in.shape[0]
    capacity = frame_count * top_count // experts
    slots = experts * capacity
    shard = exp_n * capacity
    tap_count = conv_weight.shape[0]
    half_taps = (tap_count - 1) // 2
    positions = lax.axis_index("seq") * frame_count + jnp.arange(frame_count, dtype=jnp.int32)
    live_int = (positions < lengths[0]).astype(jnp.int32)
    live_mask = live_int.astype(F32)[:, None]

    ids_local = expert_ids[0]
    matches = ids_local[:, :, None] == jnp.arange(experts, dtype=jnp.int32)[None, None, :]
    counted = (matches & (live_int == 1)[:, None, None]).astype(F32)
    counted = counted.reshape(frame_count * top_count, experts)
    pair_at = jnp.arange(frame_count * top_count)
    before = (pair_at[:, None] > pair_at[None, :]).astype(BF)
    earlier = jnp.dot(before, counted.astype(BF), preferred_element_type=F32)
    slot_index = jnp.sum(earlier * counted, axis=-1).reshape(frame_count, top_count)
    slot_index = slot_index.astype(jnp.int32)
    kept_bool = (live_int[:, None] == 1) & (slot_index < capacity)
    kept_mask = kept_bool.astype(F32)
    home_slot = jnp.sum(matches.astype(jnp.int32) * placement[None, None, :], axis=-1)
    dest_row = home_slot * capacity + slot_index
    dest_row = jnp.where(kept_bool, dest_row, -1)
    row_at = jnp.arange(slots, dtype=jnp.int32)
    chosen = dest_row[:, :, None] == row_at
    pick = jnp.any(chosen, axis=1).astype(BF)
    gates_local = gate_probs[0]
    slot_gate = jnp.sum(jnp.where(chosen, gates_local[:, :, None], 0.0), axis=(0, 1))

    def pack(values):
        return jnp.einsum("fs,fd->sd", pick, values, preferred_element_type=F32)

    def unpack(rows):
        by_k = chosen.astype(BF).transpose(1, 0, 2)
        return jnp.einsum("kfs,sd->kfd", by_k, rows, preferred_element_type=F32)

    def to_plane(rows):
        rows = swap_exp(rows.reshape(exp_n, per_dev, capacity, model_width))
        return rows.swapaxes(0, 1).reshape(per_dev, shard, model_width)

    def by_exp(own):
        return own.reshape(per_dev, exp_n, capacity, model_width).swapaxes(0, 1)

    cot = cotangent[0]
    packed_grads = (pack(cot) * slot_gate[:, None]).astype(BF)
    own_grads = to_plane(packed_grads)

    frames_f32 = frame_rows.astype(F32)
    inv_rms = lax.rsqrt(jnp.mean(frames_f32 * frames_f32, axis=-1, keepdims=True) + 1e-06)
    unit_rows = frames_f32 * inv_rms
    normed = (unit_rows * live_mask).astype(BF)
    normed = tied(normed, packed_grads)
    normed_wide = widen_rim(normed, half_taps)
    conv_out = jnp.zeros_like(frames_f32)
    for tap_index in range(tap_count):
        conv_out = (
            conv_out + normed_wide[tap_index : tap_index + frame_count] * conv_weight[tap_index]
        )
    mid_rows = (frames_f32 + live_mask * jax.nn.silu(conv_out)).astype(BF)
    packed_rows = pack(mid_rows).astype(BF)

    grad1 = gather_first(tied(own_grads, packed_rows))
    own_rows = to_plane(packed_rows)
    grad2 = gather_second(gather_second_sends(grad1))
    row1 = gather_first(own_rows)
    d_hidden1 = d_hidden_of(tied(grad1, own_rows), weight_out)
    row2_sends, grad3_sends = tied(
        (gather_second_sends(row1), (grad2[0][0], grad2[0][1])), d_hidden1
    )
    row2 = gather_second(row2_sends)
    grad3 = gather_third(grad3_sends)
    row1, grad2 = tied((row1, grad2), row2_sends, grad3_sends)
    lot1, hidden1, d_pre1 = hidden_of(row1, weight_in, d_hidden1)
    d_hidden2 = d_hidden_of(grad2, weight_out)
    row3_sends = tied((row2[0][0], row2[0][1]), d_hidden2, lot1)
    row3 = gather_third(row3_sends)
    row2, grad3 = tied((row2, grad3), row3_sends)
    lot2, hidden2, d_pre2 = hidden_of(row2, weight_in, d_hidden2)
    lot3, hidden3, d_pre3 = far_of(grad3, tied(row3, lot2), weight_in, weight_out)

    in1 = reduce_first(lot3)
    hidden1, hidden2, hidden3, row3, grad3 = tied((hidden1, hidden2, hidden3, row3, grad3), lot3)
    row3, grad3 = (jnp.stack(row3),), (jnp.stack(grad3),)
    in2_over = reduce_second_over(lot2, in1)
    lot2, hidden1, hidden2, hidden3 = tied((lot2, hidden1, hidden2, hidden3), in2_over)
    out_lot1 = out_of(hidden1, weight_out, shard)
    out_lot2 = out_of(hidden2, weight_out, shard)
    out_lot3 = out_of(hidden3, weight_out, shard)
    hiddens, d_pres = tied(((hidden1, hidden2, hidden3), (d_pre1, d_pre2, d_pre3)), in2_over)
    in2 = (cross(in2_over), *reduce_second_along(lot2))
    d_weight_out = grad_out_of((*grad1, *grad2, *grad3), hiddens)
    in3 = reduce_third(tied(lot1, d_weight_out, out_lot1, out_lot2, out_lot3), in2)
    d_weight_in = grad_in_of((*row1, *row2, *row3), tied(d_pres, in3))
    own_in = by_exp(tied(reduce_end(*in3), d_weight_in))
    rows_in = swap_exp(own_in).reshape(slots, model_width)
    out_lot1, out_lot2, out_lot3 = tied((out_lot1, out_lot2, out_lot3), own_in)
    out1 = reduce_first(out_lot3[0])
    out2 = (cross(reduce_second_over(out_lot2, out1)), *reduce_second_along(out_lot2))
    out3 = reduce_third(out_lot1, out2)

    slope = live_mask * swish_slope(conv_out)
    d_mid, d_conv, tap_grads = conv_back_of(pick, rows_in, cot, slope, normed_wide, tap_count)
    d_conv_wide = widen_rim(d_conv, half_taps)
    d_normed = jnp.zeros_like(frames_f32)
    for tap_index in range(tap_count):
        shift_at = 2 * half_taps - tap_index
        d_normed = (
            d_normed + conv_weight[tap_index] * d_conv_wide[shift_at : shift_at + frame_count]
        )
    own_out = reduce_end(*out3)
    expert_out = unpack(swap_exp(by_exp(own_out)).reshape(slots, model_width))
    tap_sums = sum_everywhere(tap_grads, out3).reshape(4, -1, model_width // 4)
    d_conv_weight = tap_sums.transpose(1, 0, 2).reshape(-1, model_width)[:tap_count]
    d_unit = d_normed * live_mask
    d_frames = (
        d_mid
        + inv_rms * (d_unit - unit_rows * jnp.mean(d_unit * unit_rows, axis=-1, keepdims=True))
    ).astype(BF)

    grad_out = cot.astype(F32)
    gates = (gates_local * kept_mask).T[:, :, None]
    mix_out = jnp.sum(gates * expert_out, axis=0)
    block_out = (mid_rows.astype(F32) + mix_out).astype(BF)
    d_gate_probs = kept_mask * jnp.sum(grad_out[None] * expert_out, axis=-1).T

    return (
        block_out[None],
        d_frames[None],
        d_gate_probs[None],
        d_conv_weight,
        d_weight_in,
        d_weight_out,
    )


def solution(mesh):
    in_specs = (
        P("exp", "seq", None),
        P(),
        P("exp", "seq", None),
        P("exp", "seq", None),
        P("exp"),
        P(),
        P("exp", None, "seq"),
        P("exp", "seq", None),
        P("exp", "seq", None),
    )
    out_specs = (
        P("exp", "seq", None),
        P("exp", "seq", None),
        P("exp", "seq", None),
        P(),
        P("exp", None, "seq"),
        P("exp", "seq", None),
    )
    return jax.shard_map(local, mesh=mesh, in_specs=in_specs, out_specs=out_specs, check_vma=False)
```

```python
import functools

import jax
import jax.numpy as jnp
from jax import lax
from jax.experimental import pallas as pl
from jax.experimental.pallas import tpu as pltpu
from jax.sharding import PartitionSpec as P

BF = jnp.bfloat16
F32 = jnp.float32


def swish_slope(value):
    sigmoid_value = jax.nn.sigmoid(value)
    return sigmoid_value + value * sigmoid_value * (1.0 - sigmoid_value)


def cross(value):
    return lax.ppermute(value, "seq", [(s, (s + 4) % 8) for s in range(8)])


def upward(value):
    return lax.ppermute(value, "seq", [(s, s // 4 * 4 + (s + 1) % 4) for s in range(8)])


def downward(value):
    return lax.ppermute(value, "seq", [(s, s // 4 * 4 + (s + 3) % 4) for s in range(8)])


def tied(values, *others):
    return lax.optimization_barrier((values, others))[0]


def gather_first(own):
    return own, cross(own), upward(own), downward(own)


def gather_second_sends(first):
    _, over, down, up = first
    return (
        jnp.stack([down[0], up[1]]),
        jnp.stack([down[0], over[1]]),
        jnp.stack([over[0], up[1]]),
    )


def gather_second(sends):
    return cross(sends[0]), upward(sends[1]), downward(sends[2])


def gather_third(sends):
    return upward(sends[0]), downward(sends[1])


def plus(*terms):
    return sum(term.astype(F32) for term in terms).astype(BF)


def reduce_first(third):
    return downward(third[0]), upward(third[1])


def reduce_second_over(second, far):
    return jnp.stack([plus(second[0][0], far[0]), plus(second[0][1], far[1])])


def reduce_second_along(second):
    return downward(second[1]), upward(second[2])


def reduce_third(first, second):
    own, over, down, up = first
    over2, down2, up2 = second
    down = jnp.stack([plus(down[0], over2[0], down2[0]), down[1]])
    up = jnp.stack([up[0], plus(up[1], over2[1], up2[1])])
    over = jnp.stack([plus(over[0], up2[0]), plus(over[1], down2[1])])
    return own, over, down, up


def reduce_end(own, over, down, up):
    return plus(own, cross(over), downward(down), upward(up))


def swap_exp(rows):
    return lax.all_to_all(rows, "exp", split_axis=0, concat_axis=0, tiled=True)


def widen_rim(field_in, half_taps):
    count = lax.axis_size("seq")
    ends = count - 1
    frame_count = field_in.shape[0]
    head, tail = field_in[:half_taps], field_in[frame_count - half_taps :]
    return jnp.concatenate(
        [
            lax.ppermute(tail, "seq", [(i, i + 1) for i in range(ends)]),
            field_in,
            lax.ppermute(head, "seq", [(i + 1, i) for i in range(ends)]),
        ],
        axis=0,
    ).astype(F32)


def send(value, axis, step):
    def target(at):
        seq, exp = divmod(at, 16)
        low, y, high, z, core = seq // 4, seq % 4, exp // 8, exp // 2 % 4, exp % 2
        x = high * 2 + low
        if axis == "x":
            x = (x + step) % 4
        elif axis == "y":
            y = (y + step) % 4
        elif axis == "z":
            z = (z + step) % 4
        else:
            core = 1 - core
        return ((x % 2) * 4 + y) * 16 + (x // 2) * 8 + z * 2 + core

    return lax.ppermute(value, ("seq", "exp"), [(at, target(at)) for at in range(128)])


def sum_everywhere(values, others):
    count = values.shape[0] // 2
    first = lax.axis_index("exp") % 2 == 0
    low, high = values[:count], values[count:]
    half = jnp.where(first, low, high) + send(jnp.where(first, high, low), "core", 1)
    for axis, before in (("z", others[0]), ("y", ()), ("x", others[1])):
        half = tied(half, before)
        half = (half + send(half, axis, 2)) + (send(half, axis, 1) + send(half, axis, 3))
    other = send(half, "core", 1)
    return jnp.concatenate([jnp.where(first, half, other), jnp.where(first, other, half)])


NT = (((1,), (1,)), ((), ()))


def cost(flops):
    return pl.CostEstimate(flops=flops // 4096, bytes_accessed=1 << 10, transcendentals=0)


def join(pieces, whole):
    shard = pieces[0].shape[1]
    for i, piece in enumerate(pieces):
        whole[i * shard : (i + 1) * shard] = piece[0]


def part_of(whole, pieces):
    shard = pieces[0].shape[1]
    for i, piece in enumerate(pieces):
        piece[0] = whole[i * shard : (i + 1) * shard].astype(BF)


def d_hidden_kernel(count, *refs):
    grads, (weight_out, d_hidden, whole) = refs[:count], refs[count:]

    @pl.when(pl.program_id(1) == 0)
    def _():
        join(grads, whole)

    d_hidden[0] = lax.dot_general(whole[...], weight_out[0], NT, preferred_element_type=F32)


def hidden_kernel(count, group, *refs):
    rows, (weight_in, d_hidden) = refs[:count], refs[count : count + 2]
    lot, (hidden_ref, d_pre_ref) = refs[count + 2 : 2 * count + 2], refs[2 * count + 2 :]
    shard = rows[0].shape[1]
    weights = weight_in[0]
    for first in range(0, count, group):
        mine = range(first, min(first + group, count))
        at = slice(first * shard, (mine[-1] + 1) * shard)
        block = jnp.concatenate([rows[i][0] for i in mine], axis=0)
        pre_act = jnp.dot(block, weights, preferred_element_type=F32)
        gate = jax.nn.sigmoid(pre_act)
        swish = pre_act * gate
        d_pre = (d_hidden[0, at] * (gate + swish * (1.0 - gate))).astype(BF)
        hidden_ref[0, at] = swish.astype(BF)
        d_pre_ref[0, at] = d_pre
        back = lax.dot_general(d_pre, weights, NT, preferred_element_type=F32).astype(BF)
        for i in mine:
            lot[i][0] = back[(i - first) * shard : (i - first + 1) * shard]


def out_kernel(count, *refs):
    hidden, weight_out = refs[:2]
    lot, total = refs[2:-1], refs[-1]
    total[...] = jnp.dot(hidden[0], weight_out[0], preferred_element_type=F32)
    part_of(total, lot)


TN = (((0,), (0,)), ((), ()))


def grad_in_kernel(count, *refs):
    rows, d_pres, (out,) = refs[:count], refs[count:-1], refs[-1:]
    left = jnp.concatenate([row[0] for row in rows], axis=0)
    right = jnp.concatenate([d_pre[0] for d_pre in d_pres], axis=0)
    out[0] = lax.dot_general(left, right, TN, preferred_element_type=F32).astype(BF)


def grad_out_kernel(count, *refs):
    grads, hiddens, (out,) = refs[:count], refs[count:-1], refs[-1:]
    left = jnp.concatenate([hidden[0] for hidden in hiddens], axis=0)
    right = jnp.concatenate([grad[0] for grad in grads], axis=0)
    out[0] = lax.dot_general(left, right, TN, preferred_element_type=F32).astype(BF)


def grad_in_of(rows, d_pres):
    count = len(rows)
    per_dev, shard, width = rows[0].shape
    units = d_pres[0].shape[2]
    return pl.pallas_call(
        functools.partial(grad_in_kernel, count),
        grid=(per_dev, width // BLOCK),
        in_specs=[pl.BlockSpec((1, shard, BLOCK), lambda e, d: (e, 0, d))] * count
        + [pl.BlockSpec((1, d_pre.shape[1], units), lambda e, d: (e, 0, 0)) for d_pre in d_pres],
        out_specs=pl.BlockSpec((1, BLOCK, units), lambda e, d: (e, d, 0)),
        out_shape=jax.ShapeDtypeStruct((per_dev, width, units), BF),
        compiler_params=LIMIT,
        cost_estimate=cost(2 * per_dev * count * shard * units * width),
        name="grad_in",
    )(*rows, *d_pres)


def grad_out_of(grads, hiddens):
    count = len(grads)
    per_dev, shard, width = grads[0].shape
    units = hiddens[0].shape[2]
    return pl.pallas_call(
        functools.partial(grad_out_kernel, count),
        grid=(per_dev, units // BLOCK),
        in_specs=[piece_spec(shard, width)] * count
        + [
            pl.BlockSpec((1, hidden.shape[1], BLOCK), lambda e, f: (e, 0, f)) for hidden in hiddens
        ],
        out_specs=pl.BlockSpec((1, BLOCK, width), lambda e, f: (e, f, 0)),
        out_shape=jax.ShapeDtypeStruct((per_dev, units, width), BF),
        compiler_params=LIMIT,
        cost_estimate=cost(2 * per_dev * count * shard * units * width),
        name="grad_out",
    )(*grads, *hiddens)


def conv_back_kernel(taps, pick, rows, cot, slope, wide, d_mid_ref, d_conv_ref, tap_ref):
    frame_count = cot.shape[0]
    d_mid = cot[...].astype(F32) + jnp.dot(pick[...], rows[...], preferred_element_type=F32)
    d_conv = (d_mid * slope[...]).astype(BF)
    d_mid_ref[...] = d_mid
    d_conv_ref[...] = d_conv
    d_conv = d_conv.astype(F32)
    tap_ref[...] = jnp.zeros_like(tap_ref)
    for tap in range(taps):
        product = d_conv * wide[tap : tap + frame_count]
        tap_ref[tap : tap + 1] = jnp.sum(product, axis=0, keepdims=True)


def conv_back_of(pick, rows, cot, slope, wide, taps):
    frame_count, width = cot.shape
    block, held = width // 4, -(-taps // 8) * 8

    def columns(array):
        return pl.BlockSpec((array.shape[0], block), lambda c: (0, c))

    return pl.pallas_call(
        functools.partial(conv_back_kernel, taps),
        grid=(4,),
        in_specs=[pl.BlockSpec(pick.shape, lambda c: (0, 0))]
        + [columns(array) for array in (rows, cot, slope, wide)],
        out_specs=[columns(cot), columns(cot), pl.BlockSpec((held, block), lambda c: (c, 0))],
        out_shape=[
            jax.ShapeDtypeStruct((frame_count, width), F32),
            jax.ShapeDtypeStruct((frame_count, width), BF),
            jax.ShapeDtypeStruct((4 * held, block), F32),
        ],
        compiler_params=LIMIT,
        cost_estimate=pl.CostEstimate(flops=1 << 20, bytes_accessed=1 << 22, transcendentals=0),
        name="conv_back",
    )(pick, rows, cot, slope, wide)


BLOCK = 256
LIMIT = pltpu.CompilerParams(vmem_limit_bytes=24 << 20)


def piece_spec(shard, width):
    return pl.BlockSpec((1, shard, width), lambda e, f: (e, 0, 0))


def d_hidden_of(grads, weight_out):
    count = len(grads)
    per_dev, shard, width = grads[0].shape
    units, total = weight_out.shape[1], count * shard
    return pl.pallas_call(
        functools.partial(d_hidden_kernel, count),
        grid=(per_dev, units // BLOCK),
        in_specs=[piece_spec(shard, width)] * count
        + [pl.BlockSpec((1, BLOCK, width), lambda e, f: (e, f, 0))],
        out_specs=pl.BlockSpec((1, total, BLOCK), lambda e, f: (e, 0, f)),
        out_shape=jax.ShapeDtypeStruct((per_dev, total, units), F32),
        scratch_shapes=[pltpu.VMEM((total, width), BF)],
        compiler_params=LIMIT,
        cost_estimate=cost(2 * per_dev * total * units * width),
        name="d_hidden",
    )(*grads, weight_out)


def hidden_of(rows, weight_in, d_hidden):
    count = len(rows)
    per_dev, shard, width = rows[0].shape
    units, total = weight_in.shape[2], count * shard
    inner = pl.BlockSpec((1, total, units), lambda e: (e, 0, 0))
    inner_shape = jax.ShapeDtypeStruct((per_dev, total, units), BF)
    piece = pl.BlockSpec((1, shard, width), lambda e: (e, 0, 0))
    outs = pl.pallas_call(
        functools.partial(hidden_kernel, count, 2),
        grid=(per_dev,),
        in_specs=[piece] * count
        + [pl.BlockSpec((1, width, units), lambda e: (e, 0, 0)), inner],
        out_specs=[piece] * count + [inner] * 2,
        out_shape=[jax.ShapeDtypeStruct((per_dev, shard, width), BF)] * count + [inner_shape] * 2,
        compiler_params=LIMIT,
        cost_estimate=cost(4 * per_dev * total * units * width),
        name="hidden",
    )(*rows, weight_in, d_hidden)
    return outs[:count], outs[count], outs[count + 1]


def far_kernel(grads0, grads1, rows0, rows1, weight_in, weight_out, lot, hidden_ref, d_pre_ref):
    first = pl.program_id(0) == 0
    grads = jnp.where(first, grads0[...], grads1[...])
    rows = jnp.where(first, rows0[...], rows1[...])
    d_hidden = lax.dot_general(grads, weight_out[0], NT, preferred_element_type=F32)
    pre_act = jnp.dot(rows, weight_in[0], preferred_element_type=F32)
    gate = jax.nn.sigmoid(pre_act)
    swish = pre_act * gate
    d_pre = (d_hidden * (gate + swish * (1.0 - gate))).astype(BF)
    hidden_ref[0] = swish.astype(BF)
    d_pre_ref[0] = d_pre
    lot[0] = lax.dot_general(d_pre, weight_in[0], NT, preferred_element_type=F32).astype(BF)


def far_of(grads, rows, weight_in, weight_out):
    shard, width = rows[0].shape
    per_dev, units = weight_out.shape[:2]

    def whole(rows_n, columns):
        return pl.BlockSpec((1, rows_n, columns), lambda e: (e, 0, 0))

    return pl.pallas_call(
        far_kernel,
        grid=(per_dev,),
        in_specs=[pl.BlockSpec((shard, width), lambda e: (0, 0))] * 4
        + [whole(width, units), whole(units, width)],
        out_specs=[whole(shard, width)] + [whole(shard, units)] * 2,
        out_shape=[jax.ShapeDtypeStruct((per_dev, shard, width), BF)]
        + [jax.ShapeDtypeStruct((per_dev, shard, units), BF)] * 2,
        compiler_params=LIMIT,
        cost_estimate=cost(6 * per_dev * shard * units * width),
        name="far",
    )(*grads, *rows, weight_in, weight_out)


def out_of(hidden, weight_out, shard):
    per_dev, total, units = hidden.shape
    width = weight_out.shape[2]
    count = total // shard
    piece = pl.BlockSpec((1, shard, width), lambda e: (e, 0, 0))
    return pl.pallas_call(
        functools.partial(out_kernel, count),
        grid=(per_dev,),
        in_specs=[
            pl.BlockSpec((1, total, units), lambda e: (e, 0, 0)),
            pl.BlockSpec((1, units, width), lambda e: (e, 0, 0)),
        ],
        out_specs=[piece] * count,
        out_shape=[jax.ShapeDtypeStruct((per_dev, shard, width), BF)] * count,
        scratch_shapes=[pltpu.VMEM((total, width), F32)],
        compiler_params=LIMIT,
        cost_estimate=cost(2 * per_dev * total * units * width),
        name="partial_out",
    )(hidden, weight_out)


def local(
    frames,
    conv_weight,
    gate_probs,
    expert_ids,
    lengths,
    placement,
    weight_in,
    weight_out,
    cotangent,
):
    exp_n = lax.axis_size("exp")
    frame_rows = frames[0]
    frame_count, model_width = frame_rows.shape
    experts = placement.shape[0]
    top_count = expert_ids.shape[2]
    per_dev = weight_in.shape[0]
    capacity = frame_count * top_count // experts
    slots = experts * capacity
    shard = exp_n * capacity
    tap_count = conv_weight.shape[0]
    half_taps = (tap_count - 1) // 2
    positions = lax.axis_index("seq") * frame_count + jnp.arange(frame_count, dtype=jnp.int32)
    live_int = (positions < lengths[0]).astype(jnp.int32)
    live_mask = live_int.astype(F32)[:, None]

    ids_local = expert_ids[0]
    matches = ids_local[:, :, None] == jnp.arange(experts, dtype=jnp.int32)[None, None, :]
    counted = (matches & (live_int == 1)[:, None, None]).astype(F32)
    counted = counted.reshape(frame_count * top_count, experts)
    pair_at = jnp.arange(frame_count * top_count)
    before = (pair_at[:, None] > pair_at[None, :]).astype(BF)
    earlier = jnp.dot(before, counted.astype(BF), preferred_element_type=F32)
    slot_index = jnp.sum(earlier * counted, axis=-1).reshape(frame_count, top_count)
    slot_index = slot_index.astype(jnp.int32)
    kept_bool = (live_int[:, None] == 1) & (slot_index < capacity)
    kept_mask = kept_bool.astype(F32)
    home_slot = jnp.sum(matches.astype(jnp.int32) * placement[None, None, :], axis=-1)
    dest_row = home_slot * capacity + slot_index
    dest_row = jnp.where(kept_bool, dest_row, -1)
    row_at = jnp.arange(slots, dtype=jnp.int32)
    chosen = dest_row[:, :, None] == row_at
    pick = jnp.any(chosen, axis=1).astype(BF)
    gates_local = gate_probs[0]
    slot_gate = jnp.sum(jnp.where(chosen, gates_local[:, :, None], 0.0), axis=(0, 1))

    def pack(values):
        return jnp.einsum("fs,fd->sd", pick, values, preferred_element_type=F32)

    def unpack(rows):
        by_k = chosen.astype(BF).transpose(1, 0, 2)
        return jnp.einsum("kfs,sd->kfd", by_k, rows, preferred_element_type=F32)

    def to_plane(rows):
        rows = swap_exp(rows.reshape(exp_n, per_dev, capacity, model_width))
        return rows.swapaxes(0, 1).reshape(per_dev, shard, model_width)

    def by_exp(own):
        return own.reshape(per_dev, exp_n, capacity, model_width).swapaxes(0, 1)

    cot = cotangent[0]
    packed_grads = (pack(cot) * slot_gate[:, None]).astype(BF)
    own_grads = to_plane(packed_grads)

    frames_f32 = frame_rows.astype(F32)
    inv_rms = lax.rsqrt(jnp.mean(frames_f32 * frames_f32, axis=-1, keepdims=True) + 1e-06)
    unit_rows = frames_f32 * inv_rms
    normed = (unit_rows * live_mask).astype(BF)
    normed = tied(normed, packed_grads)
    normed_wide = widen_rim(normed, half_taps)
    conv_out = jnp.zeros_like(frames_f32)
    for tap_index in range(tap_count):
        conv_out = (
            conv_out + normed_wide[tap_index : tap_index + frame_count] * conv_weight[tap_index]
        )
    mid_rows = (frames_f32 + live_mask * jax.nn.silu(conv_out)).astype(BF)
    packed_rows = pack(mid_rows).astype(BF)

    grad1 = gather_first(tied(own_grads, packed_rows))
    own_rows = to_plane(packed_rows)
    grad2 = gather_second(gather_second_sends(grad1))
    row1 = gather_first(own_rows)
    d_hidden1 = d_hidden_of(tied(grad1, own_rows), weight_out)
    row2_sends, grad3_sends = tied(
        (gather_second_sends(row1), (grad2[0][0], grad2[0][1])), d_hidden1
    )
    row2 = gather_second(row2_sends)
    grad3 = gather_third(grad3_sends)
    row1, grad2 = tied((row1, grad2), row2_sends, grad3_sends)
    lot1, hidden1, d_pre1 = hidden_of(row1, weight_in, d_hidden1)
    d_hidden2 = d_hidden_of(grad2, weight_out)
    row3_sends = tied((row2[0][0], row2[0][1]), d_hidden2, lot1)
    row3 = gather_third(row3_sends)
    row2, grad3 = tied((row2, grad3), row3_sends)
    lot2, hidden2, d_pre2 = hidden_of(row2, weight_in, d_hidden2)
    lot3, hidden3, d_pre3 = far_of(grad3, tied(row3, lot2), weight_in, weight_out)

    in1 = reduce_first(lot3)
    hidden1, hidden2, hidden3, row3, grad3 = tied((hidden1, hidden2, hidden3, row3, grad3), lot3)
    row3, grad3 = (jnp.stack(row3),), (jnp.stack(grad3),)
    in2_over = reduce_second_over(lot2, in1)
    lot2, hidden1, hidden2, hidden3 = tied((lot2, hidden1, hidden2, hidden3), in2_over)
    out_lot1 = out_of(hidden1, weight_out, shard)
    out_lot2 = out_of(hidden2, weight_out, shard)
    out_lot3 = out_of(hidden3, weight_out, shard)
    hiddens, d_pres = tied(((hidden1, hidden2, hidden3), (d_pre1, d_pre2, d_pre3)), in2_over)
    in2 = (cross(in2_over), *reduce_second_along(lot2))
    d_weight_out = grad_out_of((*grad1, *grad2, *grad3), hiddens)
    in3 = reduce_third(tied(lot1, d_weight_out, out_lot1, out_lot2, out_lot3), in2)
    d_weight_in = grad_in_of((*row1, *row2, *row3), tied(d_pres, in3))
    own_in = by_exp(tied(reduce_end(*in3), d_weight_in))
    rows_in = swap_exp(own_in).reshape(slots, model_width)
    out1 = reduce_first(tied(out_lot3, in3)[0])
    out_lot1, out_lot2, out1 = tied((out_lot1, out_lot2, out1), own_in)
    out2 = (cross(reduce_second_over(out_lot2, out1)), *reduce_second_along(out_lot2))
    out3 = reduce_third(out_lot1, out2)

    slope = live_mask * swish_slope(conv_out)
    d_mid, d_conv, tap_grads = conv_back_of(pick, tied(rows_in, out3), cot, slope, normed_wide, tap_count)
    own_out = reduce_end(*out3)
    expert_out = unpack(swap_exp(by_exp(own_out)).reshape(slots, model_width))
    d_conv_wide = tied(widen_rim(d_conv, half_taps), own_out)
    d_normed = jnp.zeros_like(frames_f32)
    for tap_index in range(tap_count):
        shift_at = 2 * half_taps - tap_index
        d_normed = (
            d_normed + conv_weight[tap_index] * d_conv_wide[shift_at : shift_at + frame_count]
        )
    tap_sums = sum_everywhere(tap_grads, (own_out, expert_out)).reshape(4, -1, model_width // 4)
    d_conv_weight = tap_sums.transpose(1, 0, 2).reshape(-1, model_width)[:tap_count]
    d_unit = d_normed * live_mask
    d_frames = (
        d_mid
        + inv_rms * (d_unit - unit_rows * jnp.mean(d_unit * unit_rows, axis=-1, keepdims=True))
    ).astype(BF)

    grad_out = cot.astype(F32)
    gates = (gates_local * kept_mask).T[:, :, None]
    mix_out = jnp.sum(gates * expert_out, axis=0)
    block_out = (mid_rows.astype(F32) + mix_out).astype(BF)
    d_gate_probs = kept_mask * jnp.sum(grad_out[None] * expert_out, axis=-1).T

    return (
        block_out[None],
        d_frames[None],
        d_gate_probs[None],
        d_conv_weight,
        d_weight_in,
        d_weight_out,
    )


def solution(mesh):
    in_specs = (
        P("exp", "seq", None),
        P(),
        P("exp", "seq", None),
        P("exp", "seq", None),
        P("exp"),
        P(),
        P("exp", None, "seq"),
        P("exp", "seq", None),
        P("exp", "seq", None),
    )
    out_specs = (
        P("exp", "seq", None),
        P("exp", "seq", None),
        P("exp", "seq", None),
        P(),
        P("exp", None, "seq"),
        P("exp", "seq", None),
    )
    return jax.shard_map(local, mesh=mesh, in_specs=in_specs, out_specs=out_specs, check_vma=False)
```

```python
import functools

import jax
import jax.numpy as jnp
from jax import lax
from jax.experimental import pallas as pl
from jax.experimental.pallas import tpu as pltpu
from jax.sharding import PartitionSpec as P

BF = jnp.bfloat16
F32 = jnp.float32


def swish_slope(value):
    sigmoid_value = jax.nn.sigmoid(value)
    return sigmoid_value + value * sigmoid_value * (1.0 - sigmoid_value)


def cross(value):
    return lax.ppermute(value, "seq", [(s, (s + 4) % 8) for s in range(8)])


def upward(value):
    return lax.ppermute(value, "seq", [(s, s // 4 * 4 + (s + 1) % 4) for s in range(8)])


def downward(value):
    return lax.ppermute(value, "seq", [(s, s // 4 * 4 + (s + 3) % 4) for s in range(8)])


def tied(values, *others):
    return lax.optimization_barrier((values, others))[0]


def gather_first(own):
    return own, cross(own), upward(own), downward(own)


def gather_second_sends(first):
    _, over, down, up = first
    return (
        jnp.stack([down[0], up[1]]),
        jnp.stack([down[0], over[1]]),
        jnp.stack([over[0], up[1]]),
    )


def gather_second(sends):
    return cross(sends[0]), upward(sends[1]), downward(sends[2])


def gather_third(sends):
    return upward(sends[0]), downward(sends[1])


def plus(*terms):
    return sum(term.astype(F32) for term in terms).astype(BF)


def reduce_first(third):
    return downward(third[0]), upward(third[1])


def reduce_second_over(second, far):
    return jnp.stack([plus(second[0][0], far[0]), plus(second[0][1], far[1])])


def reduce_second_along(second):
    return downward(second[1]), upward(second[2])


def reduce_third(first, second):
    own, over, down, up = first
    over2, down2, up2 = second
    down = jnp.stack([plus(down[0], over2[0], down2[0]), down[1]])
    up = jnp.stack([up[0], plus(up[1], over2[1], up2[1])])
    over = jnp.stack([plus(over[0], up2[0]), plus(over[1], down2[1])])
    return own, over, down, up


def reduce_end(own, over, down, up):
    return plus(own, cross(over), downward(down), upward(up))


def swap_exp(rows):
    return lax.all_to_all(rows, "exp", split_axis=0, concat_axis=0, tiled=True)


def widen_rim(field_in, half_taps):
    count = lax.axis_size("seq")
    ends = count - 1
    frame_count = field_in.shape[0]
    head, tail = field_in[:half_taps], field_in[frame_count - half_taps :]
    return jnp.concatenate(
        [
            lax.ppermute(tail, "seq", [(i, i + 1) for i in range(ends)]),
            field_in,
            lax.ppermute(head, "seq", [(i + 1, i) for i in range(ends)]),
        ],
        axis=0,
    ).astype(F32)


def send(value, axis, step):
    def target(at):
        seq, exp = divmod(at, 16)
        low, y, high, z, core = seq // 4, seq % 4, exp // 8, exp // 2 % 4, exp % 2
        x = high * 2 + low
        if axis == "x":
            x = (x + step) % 4
        elif axis == "y":
            y = (y + step) % 4
        elif axis == "z":
            z = (z + step) % 4
        else:
            core = 1 - core
        return ((x % 2) * 4 + y) * 16 + (x // 2) * 8 + z * 2 + core

    return lax.ppermute(value, ("seq", "exp"), [(at, target(at)) for at in range(128)])


def sum_everywhere(values, others):
    count = values.shape[0] // 2
    first = lax.axis_index("exp") % 2 == 0
    low, high = values[:count], values[count:]
    half = jnp.where(first, low, high) + send(jnp.where(first, high, low), "core", 1)
    for axis, before in (("z", others[0]), ("y", ()), ("x", others[1])):
        half = tied(half, before)
        half = (half + send(half, axis, 2)) + (send(half, axis, 1) + send(half, axis, 3))
    other = send(half, "core", 1)
    return jnp.concatenate([jnp.where(first, half, other), jnp.where(first, other, half)])


NT = (((1,), (1,)), ((), ()))


def cost(flops):
    return pl.CostEstimate(flops=flops // 4096, bytes_accessed=1 << 10, transcendentals=0)


def join(pieces, whole):
    shard = pieces[0].shape[1]
    for i, piece in enumerate(pieces):
        whole[i * shard : (i + 1) * shard] = piece[0]


def part_of(whole, pieces):
    shard = pieces[0].shape[1]
    for i, piece in enumerate(pieces):
        piece[0] = whole[i * shard : (i + 1) * shard].astype(BF)


def d_hidden_kernel(count, *refs):
    grads, (weight_out, d_hidden, whole) = refs[:count], refs[count:]

    @pl.when(pl.program_id(1) == 0)
    def _():
        join(grads, whole)

    d_hidden[0] = lax.dot_general(whole[...], weight_out[0], NT, preferred_element_type=F32)


def hidden_kernel(count, group, *refs):
    rows, (weight_in, d_hidden) = refs[:count], refs[count : count + 2]
    lot, (hidden_ref, d_pre_ref) = refs[count + 2 : 2 * count + 2], refs[2 * count + 2 :]
    shard = rows[0].shape[1]
    weights = weight_in[0]
    for first in range(0, count, group):
        mine = range(first, min(first + group, count))
        at = slice(first * shard, (mine[-1] + 1) * shard)
        block = jnp.concatenate([rows[i][0] for i in mine], axis=0)
        pre_act = jnp.dot(block, weights, preferred_element_type=F32)
        gate = jax.nn.sigmoid(pre_act)
        swish = pre_act * gate
        d_pre = (d_hidden[0, at] * (gate + swish * (1.0 - gate))).astype(BF)
        hidden_ref[0, at] = swish.astype(BF)
        d_pre_ref[0, at] = d_pre
        back = lax.dot_general(d_pre, weights, NT, preferred_element_type=F32).astype(BF)
        for i in mine:
            lot[i][0] = back[(i - first) * shard : (i - first + 1) * shard]


def out_kernel(count, *refs):
    hidden, weight_out = refs[:2]
    lot, total = refs[2:-1], refs[-1]
    total[...] = jnp.dot(hidden[0], weight_out[0], preferred_element_type=F32)
    part_of(total, lot)


TN = (((0,), (0,)), ((), ()))


def grad_in_kernel(count, *refs):
    rows, d_pres, (out,) = refs[:count], refs[count:-1], refs[-1:]
    left = jnp.concatenate([row[0] for row in rows], axis=0)
    right = jnp.concatenate([d_pre[0] for d_pre in d_pres], axis=0)
    out[0] = lax.dot_general(left, right, TN, preferred_element_type=F32).astype(BF)


def grad_out_kernel(count, *refs):
    grads, hiddens, (out,) = refs[:count], refs[count:-1], refs[-1:]
    left = jnp.concatenate([hidden[0] for hidden in hiddens], axis=0)
    right = jnp.concatenate([grad[0] for grad in grads], axis=0)
    out[0] = lax.dot_general(left, right, TN, preferred_element_type=F32).astype(BF)


def grad_in_of(rows, d_pres):
    count = len(rows)
    per_dev, shard, width = rows[0].shape
    units = d_pres[0].shape[2]
    return pl.pallas_call(
        functools.partial(grad_in_kernel, count),
        grid=(per_dev, width // BLOCK),
        in_specs=[pl.BlockSpec((1, shard, BLOCK), lambda e, d: (e, 0, d))] * count
        + [pl.BlockSpec((1, d_pre.shape[1], units), lambda e, d: (e, 0, 0)) for d_pre in d_pres],
        out_specs=pl.BlockSpec((1, BLOCK, units), lambda e, d: (e, d, 0)),
        out_shape=jax.ShapeDtypeStruct((per_dev, width, units), BF),
        compiler_params=LIMIT,
        cost_estimate=cost(2 * per_dev * count * shard * units * width),
        name="grad_in",
    )(*rows, *d_pres)


def grad_out_of(grads, hiddens):
    count = len(grads)
    per_dev, shard, width = grads[0].shape
    units = hiddens[0].shape[2]
    return pl.pallas_call(
        functools.partial(grad_out_kernel, count),
        grid=(per_dev, units // BLOCK),
        in_specs=[piece_spec(shard, width)] * count
        + [
            pl.BlockSpec((1, hidden.shape[1], BLOCK), lambda e, f: (e, 0, f)) for hidden in hiddens
        ],
        out_specs=pl.BlockSpec((1, BLOCK, width), lambda e, f: (e, f, 0)),
        out_shape=jax.ShapeDtypeStruct((per_dev, units, width), BF),
        compiler_params=LIMIT,
        cost_estimate=cost(2 * per_dev * count * shard * units * width),
        name="grad_out",
    )(*grads, *hiddens)


def conv_back_kernel(taps, pick, rows, cot, slope, wide, d_mid_ref, d_conv_ref, tap_ref):
    frame_count = cot.shape[0]
    d_mid = cot[...].astype(F32) + jnp.dot(pick[...], rows[...], preferred_element_type=F32)
    d_conv = (d_mid * slope[...]).astype(BF)
    d_mid_ref[...] = d_mid
    d_conv_ref[...] = d_conv
    d_conv = d_conv.astype(F32)
    tap_ref[...] = jnp.zeros_like(tap_ref)
    for tap in range(taps):
        product = d_conv * wide[tap : tap + frame_count]
        tap_ref[tap : tap + 1] = jnp.sum(product, axis=0, keepdims=True)


def conv_back_of(pick, rows, cot, slope, wide, taps):
    frame_count, width = cot.shape
    block, held = width // 4, -(-taps // 8) * 8

    def columns(array):
        return pl.BlockSpec((array.shape[0], block), lambda c: (0, c))

    return pl.pallas_call(
        functools.partial(conv_back_kernel, taps),
        grid=(4,),
        in_specs=[pl.BlockSpec(pick.shape, lambda c: (0, 0))]
        + [columns(array) for array in (rows, cot, slope, wide)],
        out_specs=[columns(cot), columns(cot), pl.BlockSpec((held, block), lambda c: (c, 0))],
        out_shape=[
            jax.ShapeDtypeStruct((frame_count, width), F32),
            jax.ShapeDtypeStruct((frame_count, width), BF),
            jax.ShapeDtypeStruct((4 * held, block), F32),
        ],
        compiler_params=LIMIT,
        cost_estimate=pl.CostEstimate(flops=1 << 20, bytes_accessed=1 << 22, transcendentals=0),
        name="conv_back",
    )(pick, rows, cot, slope, wide)


BLOCK = 256
LIMIT = pltpu.CompilerParams(vmem_limit_bytes=20 << 20)


def piece_spec(shard, width):
    return pl.BlockSpec((1, shard, width), lambda e, f: (e, 0, 0))


def d_hidden_of(grads, weight_out):
    count = len(grads)
    per_dev, shard, width = grads[0].shape
    units, total = weight_out.shape[1], count * shard
    return pl.pallas_call(
        functools.partial(d_hidden_kernel, count),
        grid=(per_dev, units // BLOCK),
        in_specs=[piece_spec(shard, width)] * count
        + [pl.BlockSpec((1, BLOCK, width), lambda e, f: (e, f, 0))],
        out_specs=pl.BlockSpec((1, total, BLOCK), lambda e, f: (e, 0, f)),
        out_shape=jax.ShapeDtypeStruct((per_dev, total, units), F32),
        scratch_shapes=[pltpu.VMEM((total, width), BF)],
        compiler_params=LIMIT,
        cost_estimate=cost(2 * per_dev * total * units * width),
        name="d_hidden",
    )(*grads, weight_out)


def hidden_of(rows, weight_in, d_hidden):
    count = len(rows)
    per_dev, shard, width = rows[0].shape
    units, total = weight_in.shape[2], count * shard
    inner = pl.BlockSpec((1, total, units), lambda e: (e, 0, 0))
    inner_shape = jax.ShapeDtypeStruct((per_dev, total, units), BF)
    piece = pl.BlockSpec((1, shard, width), lambda e: (e, 0, 0))
    outs = pl.pallas_call(
        functools.partial(hidden_kernel, count, 2),
        grid=(per_dev,),
        in_specs=[piece] * count
        + [pl.BlockSpec((1, width, units), lambda e: (e, 0, 0)), inner],
        out_specs=[piece] * count + [inner] * 2,
        out_shape=[jax.ShapeDtypeStruct((per_dev, shard, width), BF)] * count + [inner_shape] * 2,
        compiler_params=LIMIT,
        cost_estimate=cost(4 * per_dev * total * units * width),
        name="hidden",
    )(*rows, weight_in, d_hidden)
    return outs[:count], outs[count], outs[count + 1]


def far_kernel(grads0, grads1, rows0, rows1, weight_in, weight_out, lot, hidden_ref, d_pre_ref):
    first = pl.program_id(0) == 0
    grads = jnp.where(first, grads0[...], grads1[...])
    rows = jnp.where(first, rows0[...], rows1[...])
    d_hidden = lax.dot_general(grads, weight_out[0], NT, preferred_element_type=F32)
    pre_act = jnp.dot(rows, weight_in[0], preferred_element_type=F32)
    gate = jax.nn.sigmoid(pre_act)
    swish = pre_act * gate
    d_pre = (d_hidden * (gate + swish * (1.0 - gate))).astype(BF)
    hidden_ref[0] = swish.astype(BF)
    d_pre_ref[0] = d_pre
    lot[0] = lax.dot_general(d_pre, weight_in[0], NT, preferred_element_type=F32).astype(BF)


def far_of(grads, rows, weight_in, weight_out):
    shard, width = rows[0].shape
    per_dev, units = weight_out.shape[:2]

    def whole(rows_n, columns):
        return pl.BlockSpec((1, rows_n, columns), lambda e: (e, 0, 0))

    return pl.pallas_call(
        far_kernel,
        grid=(per_dev,),
        in_specs=[pl.BlockSpec((shard, width), lambda e: (0, 0))] * 4
        + [whole(width, units), whole(units, width)],
        out_specs=[whole(shard, width)] + [whole(shard, units)] * 2,
        out_shape=[jax.ShapeDtypeStruct((per_dev, shard, width), BF)]
        + [jax.ShapeDtypeStruct((per_dev, shard, units), BF)] * 2,
        compiler_params=LIMIT,
        cost_estimate=cost(6 * per_dev * shard * units * width),
        name="far",
    )(*grads, *rows, weight_in, weight_out)


def out_of(hidden, weight_out, shard):
    per_dev, total, units = hidden.shape
    width = weight_out.shape[2]
    count = total // shard
    piece = pl.BlockSpec((1, shard, width), lambda e: (e, 0, 0))
    return pl.pallas_call(
        functools.partial(out_kernel, count),
        grid=(per_dev,),
        in_specs=[
            pl.BlockSpec((1, total, units), lambda e: (e, 0, 0)),
            pl.BlockSpec((1, units, width), lambda e: (e, 0, 0)),
        ],
        out_specs=[piece] * count,
        out_shape=[jax.ShapeDtypeStruct((per_dev, shard, width), BF)] * count,
        scratch_shapes=[pltpu.VMEM((total, width), F32)],
        compiler_params=LIMIT,
        cost_estimate=cost(2 * per_dev * total * units * width),
        name="partial_out",
    )(hidden, weight_out)


def local(
    frames,
    conv_weight,
    gate_probs,
    expert_ids,
    lengths,
    placement,
    weight_in,
    weight_out,
    cotangent,
):
    exp_n = lax.axis_size("exp")
    frame_rows = frames[0]
    frame_count, model_width = frame_rows.shape
    experts = placement.shape[0]
    top_count = expert_ids.shape[2]
    per_dev = weight_in.shape[0]
    capacity = frame_count * top_count // experts
    slots = experts * capacity
    shard = exp_n * capacity
    tap_count = conv_weight.shape[0]
    half_taps = (tap_count - 1) // 2
    positions = lax.axis_index("seq") * frame_count + jnp.arange(frame_count, dtype=jnp.int32)
    live_int = (positions < lengths[0]).astype(jnp.int32)
    live_mask = live_int.astype(F32)[:, None]

    ids_local = expert_ids[0]
    matches = ids_local[:, :, None] == jnp.arange(experts, dtype=jnp.int32)[None, None, :]
    counted = (matches & (live_int == 1)[:, None, None]).astype(F32)
    counted = counted.reshape(frame_count * top_count, experts)
    pair_at = jnp.arange(frame_count * top_count)
    before = (pair_at[:, None] > pair_at[None, :]).astype(BF)
    earlier = jnp.dot(before, counted.astype(BF), preferred_element_type=F32)
    slot_index = jnp.sum(earlier * counted, axis=-1).reshape(frame_count, top_count)
    slot_index = slot_index.astype(jnp.int32)
    kept_bool = (live_int[:, None] == 1) & (slot_index < capacity)
    kept_mask = kept_bool.astype(F32)
    home_slot = jnp.sum(matches.astype(jnp.int32) * placement[None, None, :], axis=-1)
    dest_row = home_slot * capacity + slot_index
    dest_row = jnp.where(kept_bool, dest_row, -1)
    row_at = jnp.arange(slots, dtype=jnp.int32)
    chosen = dest_row[:, :, None] == row_at
    pick = jnp.any(chosen, axis=1).astype(BF)
    gates_local = gate_probs[0]
    slot_gate = jnp.sum(jnp.where(chosen, gates_local[:, :, None], 0.0), axis=(0, 1))

    def pack(values):
        return jnp.einsum("fs,fd->sd", pick, values, preferred_element_type=F32)

    def unpack(rows):
        by_k = chosen.astype(BF).transpose(1, 0, 2)
        return jnp.einsum("kfs,sd->kfd", by_k, rows, preferred_element_type=F32)

    def to_plane(rows):
        rows = swap_exp(rows.reshape(exp_n, per_dev, capacity, model_width))
        return rows.swapaxes(0, 1).reshape(per_dev, shard, model_width)

    def by_exp(own):
        return own.reshape(per_dev, exp_n, capacity, model_width).swapaxes(0, 1)

    cot = cotangent[0]
    packed_grads = (pack(cot) * slot_gate[:, None]).astype(BF)
    own_grads = to_plane(packed_grads)

    frames_f32 = frame_rows.astype(F32)
    inv_rms = lax.rsqrt(jnp.mean(frames_f32 * frames_f32, axis=-1, keepdims=True) + 1e-06)
    unit_rows = frames_f32 * inv_rms
    normed = (unit_rows * live_mask).astype(BF)
    normed = tied(normed, packed_grads)
    normed_wide = widen_rim(normed, half_taps)
    conv_out = jnp.zeros_like(frames_f32)
    for tap_index in range(tap_count):
        conv_out = (
            conv_out + normed_wide[tap_index : tap_index + frame_count] * conv_weight[tap_index]
        )
    mid_rows = (frames_f32 + live_mask * jax.nn.silu(conv_out)).astype(BF)
    packed_rows = pack(mid_rows).astype(BF)

    grad1 = gather_first(tied(own_grads, packed_rows))
    own_rows = to_plane(packed_rows)
    grad2 = gather_second(gather_second_sends(grad1))
    row1 = gather_first(own_rows)
    d_hidden1 = d_hidden_of(tied(grad1, own_rows), weight_out)
    row2_sends, grad3_sends = tied(
        (gather_second_sends(row1), (grad2[0][0], grad2[0][1])), d_hidden1
    )
    row2 = gather_second(row2_sends)
    grad3 = gather_third(grad3_sends)
    row1, grad2 = tied((row1, grad2), row2_sends, grad3_sends)
    lot1, hidden1, d_pre1 = hidden_of(row1, weight_in, d_hidden1)
    d_hidden2 = d_hidden_of(grad2, weight_out)
    row3_sends = tied((row2[0][0], row2[0][1]), d_hidden2, lot1)
    row3 = gather_third(row3_sends)
    row2, grad3 = tied((row2, grad3), row3_sends)
    lot2, hidden2, d_pre2 = hidden_of(row2, weight_in, d_hidden2)
    lot3, hidden3, d_pre3 = far_of(grad3, tied(row3, lot2), weight_in, weight_out)

    in1 = reduce_first(lot3)
    hidden1, hidden2, hidden3, row3, grad3 = tied((hidden1, hidden2, hidden3, row3, grad3), lot3)
    row3, grad3 = (jnp.stack(row3),), (jnp.stack(grad3),)
    out_lot1 = out_of(hidden1, weight_out, shard)
    out_lot2 = out_of(hidden2, weight_out, shard)
    out_lot3 = out_of(hidden3, weight_out, shard)
    in2_over = reduce_second_over(lot2, tied(in1, out_lot1, out_lot2, out_lot3))
    lot2 = tied(lot2, in2_over)
    hiddens, d_pres = tied(((hidden1, hidden2, hidden3), (d_pre1, d_pre2, d_pre3)), in2_over)
    in2 = (cross(in2_over), *reduce_second_along(lot2))
    d_weight_out = grad_out_of((*grad1, *grad2, *grad3), hiddens)
    in3 = reduce_third(tied(lot1, d_weight_out, out_lot1, out_lot2, out_lot3), in2)
    d_weight_in = grad_in_of((*row1, *row2, *row3), tied(d_pres, in3))
    own_in = by_exp(tied(reduce_end(*in3), d_weight_in))
    rows_in = swap_exp(own_in).reshape(slots, model_width)
    out1 = reduce_first(tied(out_lot3, in3)[0])
    out_lot1, out_lot2, out1 = tied((out_lot1, out_lot2, out1), own_in)
    out2 = (cross(reduce_second_over(out_lot2, out1)), *reduce_second_along(out_lot2))
    out3 = reduce_third(out_lot1, out2)

    slope = live_mask * swish_slope(conv_out)
    d_mid, d_conv, tap_grads = conv_back_of(pick, tied(rows_in, out3), cot, slope, normed_wide, tap_count)
    own_out = reduce_end(*out3)
    expert_out = unpack(swap_exp(by_exp(own_out)).reshape(slots, model_width))
    d_conv_wide = tied(widen_rim(d_conv, half_taps), own_out)
    d_normed = jnp.zeros_like(frames_f32)
    for tap_index in range(tap_count):
        shift_at = 2 * half_taps - tap_index
        d_normed = (
            d_normed + conv_weight[tap_index] * d_conv_wide[shift_at : shift_at + frame_count]
        )
    tap_sums = sum_everywhere(tap_grads, (own_out, expert_out)).reshape(4, -1, model_width // 4)
    d_conv_weight = tap_sums.transpose(1, 0, 2).reshape(-1, model_width)[:tap_count]
    d_unit = d_normed * live_mask
    d_frames = (
        d_mid
        + inv_rms * (d_unit - unit_rows * jnp.mean(d_unit * unit_rows, axis=-1, keepdims=True))
    ).astype(BF)

    grad_out = cot.astype(F32)
    gates = (gates_local * kept_mask).T[:, :, None]
    mix_out = jnp.sum(gates * expert_out, axis=0)
    block_out = (mid_rows.astype(F32) + mix_out).astype(BF)
    d_gate_probs = kept_mask * jnp.sum(grad_out[None] * expert_out, axis=-1).T

    return (
        block_out[None],
        d_frames[None],
        d_gate_probs[None],
        d_conv_weight,
        d_weight_in,
        d_weight_out,
    )


def solution(mesh):
    in_specs = (
        P("exp", "seq", None),
        P(),
        P("exp", "seq", None),
        P("exp", "seq", None),
        P("exp"),
        P(),
        P("exp", None, "seq"),
        P("exp", "seq", None),
        P("exp", "seq", None),
    )
    out_specs = (
        P("exp", "seq", None),
        P("exp", "seq", None),
        P("exp", "seq", None),
        P(),
        P("exp", None, "seq"),
        P("exp", "seq", None),
    )
    return jax.shard_map(local, mesh=mesh, in_specs=in_specs, out_specs=out_specs, check_vma=False)
```

```python
import functools

import jax
import jax.numpy as jnp
from jax import lax
from jax.experimental import pallas as pl
from jax.experimental.pallas import tpu as pltpu
from jax.sharding import PartitionSpec as P

BF = jnp.bfloat16
F32 = jnp.float32


def swish_slope(value):
    sigmoid_value = jax.nn.sigmoid(value)
    return sigmoid_value + value * sigmoid_value * (1.0 - sigmoid_value)


def cross(value):
    return lax.ppermute(value, "seq", [(s, (s + 4) % 8) for s in range(8)])


def upward(value):
    return lax.ppermute(value, "seq", [(s, s // 4 * 4 + (s + 1) % 4) for s in range(8)])


def downward(value):
    return lax.ppermute(value, "seq", [(s, s // 4 * 4 + (s + 3) % 4) for s in range(8)])


def tied(values, *others):
    return lax.optimization_barrier((values, others))[0]


def gather_first(own):
    return own, cross(own), upward(own), downward(own)


def gather_second_sends(first):
    _, over, down, up = first
    return (
        jnp.stack([down[0], up[1]]),
        jnp.stack([down[0], over[1]]),
        jnp.stack([over[0], up[1]]),
    )


def gather_second(sends):
    return cross(sends[0]), upward(sends[1]), downward(sends[2])


def gather_third(sends):
    return upward(sends[0]), downward(sends[1])


def plus(*terms):
    return sum(term.astype(F32) for term in terms).astype(BF)


def reduce_first(third):
    return downward(third[0]), upward(third[1])


def reduce_second_over(second, far):
    return jnp.stack([plus(second[0][0], far[0]), plus(second[0][1], far[1])])


def reduce_second_along(second):
    return downward(second[1]), upward(second[2])


def reduce_third(first, second):
    own, over, down, up = first
    over2, down2, up2 = second
    down = jnp.stack([plus(down[0], over2[0], down2[0]), down[1]])
    up = jnp.stack([up[0], plus(up[1], over2[1], up2[1])])
    over = jnp.stack([plus(over[0], up2[0]), plus(over[1], down2[1])])
    return own, over, down, up


def reduce_end(own, over, down, up):
    return plus(own, cross(over), downward(down), upward(up))


def swap_exp(rows):
    return lax.all_to_all(rows, "exp", split_axis=0, concat_axis=0, tiled=True)


def widen_rim(field_in, half_taps):
    count = lax.axis_size("seq")
    ends = count - 1
    frame_count = field_in.shape[0]
    head, tail = field_in[:half_taps], field_in[frame_count - half_taps :]
    return jnp.concatenate(
        [
            lax.ppermute(tail, "seq", [(i, i + 1) for i in range(ends)]),
            field_in,
            lax.ppermute(head, "seq", [(i + 1, i) for i in range(ends)]),
        ],
        axis=0,
    ).astype(F32)


def send(value, axis, step):
    def target(at):
        seq, exp = divmod(at, 16)
        low, y, high, z, core = seq // 4, seq % 4, exp // 8, exp // 2 % 4, exp % 2
        x = high * 2 + low
        if axis == "x":
            x = (x + step) % 4
        elif axis == "y":
            y = (y + step) % 4
        elif axis == "z":
            z = (z + step) % 4
        else:
            core = 1 - core
        return ((x % 2) * 4 + y) * 16 + (x // 2) * 8 + z * 2 + core

    return lax.ppermute(value, ("seq", "exp"), [(at, target(at)) for at in range(128)])


def sum_everywhere(values, others):
    count = values.shape[0] // 2
    first = lax.axis_index("exp") % 2 == 0
    low, high = values[:count], values[count:]
    half = jnp.where(first, low, high) + send(jnp.where(first, high, low), "core", 1)
    for axis, before in (("z", others[0]), ("y", ()), ("x", ())):
        half = tied(half, before)
        half = (half + send(half, axis, 2)) + (send(half, axis, 1) + send(half, axis, 3))
    other = send(tied(half, others[1]), "core", 1)
    return jnp.concatenate([jnp.where(first, half, other), jnp.where(first, other, half)])


NT = (((1,), (1,)), ((), ()))


def cost(flops):
    return pl.CostEstimate(flops=flops // 4096, bytes_accessed=1 << 10, transcendentals=0)


def join(pieces, whole):
    shard = pieces[0].shape[1]
    for i, piece in enumerate(pieces):
        whole[i * shard : (i + 1) * shard] = piece[0]


def part_of(whole, pieces):
    shard = pieces[0].shape[1]
    for i, piece in enumerate(pieces):
        piece[0] = whole[i * shard : (i + 1) * shard].astype(BF)


def d_hidden_kernel(count, *refs):
    grads, (weight_out, d_hidden, whole) = refs[:count], refs[count:]

    @pl.when(pl.program_id(1) == 0)
    def _():
        join(grads, whole)

    d_hidden[0] = lax.dot_general(whole[...], weight_out[0], NT, preferred_element_type=F32)


def hidden_kernel(count, group, *refs):
    rows, (weight_in, d_hidden) = refs[:count], refs[count : count + 2]
    lot, (hidden_ref, d_pre_ref) = refs[count + 2 : 2 * count + 2], refs[2 * count + 2 :]
    shard = rows[0].shape[1]
    weights = weight_in[0]
    for first in range(0, count, group):
        mine = range(first, min(first + group, count))
        at = slice(first * shard, (mine[-1] + 1) * shard)
        block = jnp.concatenate([rows[i][0] for i in mine], axis=0)
        pre_act = jnp.dot(block, weights, preferred_element_type=F32)
        gate = jax.nn.sigmoid(pre_act)
        swish = pre_act * gate
        d_pre = (d_hidden[0, at] * (gate + swish * (1.0 - gate))).astype(BF)
        hidden_ref[0, at] = swish.astype(BF)
        d_pre_ref[0, at] = d_pre
        back = lax.dot_general(d_pre, weights, NT, preferred_element_type=F32).astype(BF)
        for i in mine:
            lot[i][0] = back[(i - first) * shard : (i - first + 1) * shard]


def out_kernel(count, *refs):
    hidden, weight_out = refs[:2]
    lot, total = refs[2:-1], refs[-1]
    total[...] = jnp.dot(hidden[0], weight_out[0], preferred_element_type=F32)
    part_of(total, lot)


TN = (((0,), (0,)), ((), ()))


def grad_in_kernel(count, *refs):
    rows, d_pres, (out,) = refs[:count], refs[count:-1], refs[-1:]
    left = jnp.concatenate([row[0] for row in rows], axis=0)
    right = jnp.concatenate([d_pre[0] for d_pre in d_pres], axis=0)
    out[0] = lax.dot_general(left, right, TN, preferred_element_type=F32).astype(BF)


def grad_out_kernel(count, *refs):
    grads, hiddens, (out,) = refs[:count], refs[count:-1], refs[-1:]
    left = jnp.concatenate([hidden[0] for hidden in hiddens], axis=0)
    right = jnp.concatenate([grad[0] for grad in grads], axis=0)
    out[0] = lax.dot_general(left, right, TN, preferred_element_type=F32).astype(BF)


def grad_in_of(rows, d_pres):
    count = len(rows)
    per_dev, shard, width = rows[0].shape
    units = d_pres[0].shape[2]
    return pl.pallas_call(
        functools.partial(grad_in_kernel, count),
        grid=(per_dev, width // BLOCK),
        in_specs=[pl.BlockSpec((1, shard, BLOCK), lambda e, d: (e, 0, d))] * count
        + [pl.BlockSpec((1, d_pre.shape[1], units), lambda e, d: (e, 0, 0)) for d_pre in d_pres],
        out_specs=pl.BlockSpec((1, BLOCK, units), lambda e, d: (e, d, 0)),
        out_shape=jax.ShapeDtypeStruct((per_dev, width, units), BF),
        compiler_params=LIMIT,
        cost_estimate=cost(2 * per_dev * count * shard * units * width),
        name="grad_in",
    )(*rows, *d_pres)


def grad_out_of(grads, hiddens):
    count = len(grads)
    per_dev, shard, width = grads[0].shape
    units = hiddens[0].shape[2]
    return pl.pallas_call(
        functools.partial(grad_out_kernel, count),
        grid=(per_dev, units // BLOCK),
        in_specs=[piece_spec(shard, width)] * count
        + [
            pl.BlockSpec((1, hidden.shape[1], BLOCK), lambda e, f: (e, 0, f)) for hidden in hiddens
        ],
        out_specs=pl.BlockSpec((1, BLOCK, width), lambda e, f: (e, f, 0)),
        out_shape=jax.ShapeDtypeStruct((per_dev, units, width), BF),
        compiler_params=LIMIT,
        cost_estimate=cost(2 * per_dev * count * shard * units * width),
        name="grad_out",
    )(*grads, *hiddens)


def conv_back_kernel(taps, pick, rows, cot, slope, wide, d_mid_ref, d_conv_ref, tap_ref):
    frame_count = cot.shape[0]
    d_mid = cot[...].astype(F32) + jnp.dot(pick[...], rows[...], preferred_element_type=F32)
    d_conv = (d_mid * slope[...]).astype(BF)
    d_mid_ref[...] = d_mid
    d_conv_ref[...] = d_conv
    d_conv = d_conv.astype(F32)
    tap_ref[...] = jnp.zeros_like(tap_ref)
    for tap in range(taps):
        product = d_conv * wide[tap : tap + frame_count]
        tap_ref[tap : tap + 1] = jnp.sum(product, axis=0, keepdims=True)


def conv_back_of(pick, rows, cot, slope, wide, taps):
    frame_count, width = cot.shape
    block, held = width // 4, -(-taps // 8) * 8

    def columns(array):
        return pl.BlockSpec((array.shape[0], block), lambda c: (0, c))

    return pl.pallas_call(
        functools.partial(conv_back_kernel, taps),
        grid=(4,),
        in_specs=[pl.BlockSpec(pick.shape, lambda c: (0, 0))]
        + [columns(array) for array in (rows, cot, slope, wide)],
        out_specs=[columns(cot), columns(cot), pl.BlockSpec((held, block), lambda c: (c, 0))],
        out_shape=[
            jax.ShapeDtypeStruct((frame_count, width), F32),
            jax.ShapeDtypeStruct((frame_count, width), BF),
            jax.ShapeDtypeStruct((4 * held, block), F32),
        ],
        compiler_params=LIMIT,
        cost_estimate=pl.CostEstimate(flops=1 << 20, bytes_accessed=1 << 22, transcendentals=0),
        name="conv_back",
    )(pick, rows, cot, slope, wide)


BLOCK = 256
LIMIT = pltpu.CompilerParams(vmem_limit_bytes=20 << 20)


def piece_spec(shard, width):
    return pl.BlockSpec((1, shard, width), lambda e, f: (e, 0, 0))


def d_hidden_of(grads, weight_out):
    count = len(grads)
    per_dev, shard, width = grads[0].shape
    units, total = weight_out.shape[1], count * shard
    return pl.pallas_call(
        functools.partial(d_hidden_kernel, count),
        grid=(per_dev, units // BLOCK),
        in_specs=[piece_spec(shard, width)] * count
        + [pl.BlockSpec((1, BLOCK, width), lambda e, f: (e, f, 0))],
        out_specs=pl.BlockSpec((1, total, BLOCK), lambda e, f: (e, 0, f)),
        out_shape=jax.ShapeDtypeStruct((per_dev, total, units), F32),
        scratch_shapes=[pltpu.VMEM((total, width), BF)],
        compiler_params=LIMIT,
        cost_estimate=cost(2 * per_dev * total * units * width),
        name="d_hidden",
    )(*grads, weight_out)


def hidden_of(rows, weight_in, d_hidden):
    count = len(rows)
    per_dev, shard, width = rows[0].shape
    units, total = weight_in.shape[2], count * shard
    inner = pl.BlockSpec((1, total, units), lambda e: (e, 0, 0))
    inner_shape = jax.ShapeDtypeStruct((per_dev, total, units), BF)
    piece = pl.BlockSpec((1, shard, width), lambda e: (e, 0, 0))
    outs = pl.pallas_call(
        functools.partial(hidden_kernel, count, 2),
        grid=(per_dev,),
        in_specs=[piece] * count
        + [pl.BlockSpec((1, width, units), lambda e: (e, 0, 0)), inner],
        out_specs=[piece] * count + [inner] * 2,
        out_shape=[jax.ShapeDtypeStruct((per_dev, shard, width), BF)] * count + [inner_shape] * 2,
        compiler_params=LIMIT,
        cost_estimate=cost(4 * per_dev * total * units * width),
        name="hidden",
    )(*rows, weight_in, d_hidden)
    return outs[:count], outs[count], outs[count + 1]


def far_kernel(grads0, grads1, rows0, rows1, weight_in, weight_out, lot, hidden_ref, d_pre_ref):
    first = pl.program_id(0) == 0
    grads = jnp.where(first, grads0[...], grads1[...])
    rows = jnp.where(first, rows0[...], rows1[...])
    d_hidden = lax.dot_general(grads, weight_out[0], NT, preferred_element_type=F32)
    pre_act = jnp.dot(rows, weight_in[0], preferred_element_type=F32)
    gate = jax.nn.sigmoid(pre_act)
    swish = pre_act * gate
    d_pre = (d_hidden * (gate + swish * (1.0 - gate))).astype(BF)
    hidden_ref[0] = swish.astype(BF)
    d_pre_ref[0] = d_pre
    lot[0] = lax.dot_general(d_pre, weight_in[0], NT, preferred_element_type=F32).astype(BF)


def far_of(grads, rows, weight_in, weight_out):
    shard, width = rows[0].shape
    per_dev, units = weight_out.shape[:2]

    def whole(rows_n, columns):
        return pl.BlockSpec((1, rows_n, columns), lambda e: (e, 0, 0))

    return pl.pallas_call(
        far_kernel,
        grid=(per_dev,),
        in_specs=[pl.BlockSpec((shard, width), lambda e: (0, 0))] * 4
        + [whole(width, units), whole(units, width)],
        out_specs=[whole(shard, width)] + [whole(shard, units)] * 2,
        out_shape=[jax.ShapeDtypeStruct((per_dev, shard, width), BF)]
        + [jax.ShapeDtypeStruct((per_dev, shard, units), BF)] * 2,
        compiler_params=LIMIT,
        cost_estimate=cost(6 * per_dev * shard * units * width),
        name="far",
    )(*grads, *rows, weight_in, weight_out)


def out_of(hidden, weight_out, shard):
    per_dev, total, units = hidden.shape
    width = weight_out.shape[2]
    count = total // shard
    piece = pl.BlockSpec((1, shard, width), lambda e: (e, 0, 0))
    return pl.pallas_call(
        functools.partial(out_kernel, count),
        grid=(per_dev,),
        in_specs=[
            pl.BlockSpec((1, total, units), lambda e: (e, 0, 0)),
            pl.BlockSpec((1, units, width), lambda e: (e, 0, 0)),
        ],
        out_specs=[piece] * count,
        out_shape=[jax.ShapeDtypeStruct((per_dev, shard, width), BF)] * count,
        scratch_shapes=[pltpu.VMEM((total, width), F32)],
        compiler_params=LIMIT,
        cost_estimate=cost(2 * per_dev * total * units * width),
        name="partial_out",
    )(hidden, weight_out)


def local(
    frames,
    conv_weight,
    gate_probs,
    expert_ids,
    lengths,
    placement,
    weight_in,
    weight_out,
    cotangent,
):
    exp_n = lax.axis_size("exp")
    frame_rows = frames[0]
    frame_count, model_width = frame_rows.shape
    experts = placement.shape[0]
    top_count = expert_ids.shape[2]
    per_dev = weight_in.shape[0]
    capacity = frame_count * top_count // experts
    slots = experts * capacity
    shard = exp_n * capacity
    tap_count = conv_weight.shape[0]
    half_taps = (tap_count - 1) // 2
    positions = lax.axis_index("seq") * frame_count + jnp.arange(frame_count, dtype=jnp.int32)
    live_int = (positions < lengths[0]).astype(jnp.int32)
    live_mask = live_int.astype(F32)[:, None]

    ids_local = expert_ids[0]
    matches = ids_local[:, :, None] == jnp.arange(experts, dtype=jnp.int32)[None, None, :]
    counted = (matches & (live_int == 1)[:, None, None]).astype(F32)
    counted = counted.reshape(frame_count * top_count, experts)
    pair_at = jnp.arange(frame_count * top_count)
    before = (pair_at[:, None] > pair_at[None, :]).astype(BF)
    earlier = jnp.dot(before, counted.astype(BF), preferred_element_type=F32)
    slot_index = jnp.sum(earlier * counted, axis=-1).reshape(frame_count, top_count)
    slot_index = slot_index.astype(jnp.int32)
    kept_bool = (live_int[:, None] == 1) & (slot_index < capacity)
    kept_mask = kept_bool.astype(F32)
    home_slot = jnp.sum(matches.astype(jnp.int32) * placement[None, None, :], axis=-1)
    dest_row = home_slot * capacity + slot_index
    dest_row = jnp.where(kept_bool, dest_row, -1)
    row_at = jnp.arange(slots, dtype=jnp.int32)
    chosen = dest_row[:, :, None] == row_at
    pick = jnp.any(chosen, axis=1).astype(BF)
    gates_local = gate_probs[0]
    slot_gate = jnp.sum(jnp.where(chosen, gates_local[:, :, None], 0.0), axis=(0, 1))

    def pack(values):
        return jnp.einsum("fs,fd->sd", pick, values, preferred_element_type=F32)

    def unpack(rows):
        by_k = chosen.astype(BF).transpose(1, 0, 2)
        return jnp.einsum("kfs,sd->kfd", by_k, rows, preferred_element_type=F32)

    def to_plane(rows):
        rows = swap_exp(rows.reshape(exp_n, per_dev, capacity, model_width))
        return rows.swapaxes(0, 1).reshape(per_dev, shard, model_width)

    def by_exp(own):
        return own.reshape(per_dev, exp_n, capacity, model_width).swapaxes(0, 1)

    cot = cotangent[0]
    packed_grads = (pack(cot) * slot_gate[:, None]).astype(BF)
    own_grads = to_plane(packed_grads)

    frames_f32 = frame_rows.astype(F32)
    inv_rms = lax.rsqrt(jnp.mean(frames_f32 * frames_f32, axis=-1, keepdims=True) + 1e-06)
    unit_rows = frames_f32 * inv_rms
    normed = (unit_rows * live_mask).astype(BF)
    normed = tied(normed, packed_grads)
    normed_wide = widen_rim(normed, half_taps)
    conv_out = jnp.zeros_like(frames_f32)
    for tap_index in range(tap_count):
        conv_out = (
            conv_out + normed_wide[tap_index : tap_index + frame_count] * conv_weight[tap_index]
        )
    mid_rows = (frames_f32 + live_mask * jax.nn.silu(conv_out)).astype(BF)
    packed_rows = pack(mid_rows).astype(BF)

    grad1 = gather_first(tied(own_grads, packed_rows))
    own_rows = to_plane(packed_rows)
    grad2 = gather_second(gather_second_sends(grad1))
    row1 = gather_first(own_rows)
    d_hidden1 = d_hidden_of(tied(grad1, own_rows), weight_out)
    row2_sends, grad3_sends = tied(
        (gather_second_sends(row1), (grad2[0][0], grad2[0][1])), d_hidden1
    )
    row2 = gather_second(row2_sends)
    grad3 = gather_third(grad3_sends)
    row1, grad2 = tied((row1, grad2), row2_sends, grad3_sends)
    lot1, hidden1, d_pre1 = hidden_of(row1, weight_in, d_hidden1)
    d_hidden2 = d_hidden_of(grad2, weight_out)
    row3_sends = tied((row2[0][0], row2[0][1]), d_hidden2, lot1)
    row3 = gather_third(row3_sends)
    row2, grad3 = tied((row2, grad3), row3_sends)
    lot2, hidden2, d_pre2 = hidden_of(row2, weight_in, d_hidden2)
    lot3, hidden3, d_pre3 = far_of(grad3, tied(row3, lot2), weight_in, weight_out)

    in1 = reduce_first(lot3)
    hidden1, hidden2, hidden3, row3, grad3 = tied((hidden1, hidden2, hidden3, row3, grad3), lot3)
    row3, grad3 = (jnp.stack(row3),), (jnp.stack(grad3),)
    out_lot1 = out_of(hidden1, weight_out, shard)
    out_lot2 = out_of(hidden2, weight_out, shard)
    out_lot3 = out_of(hidden3, weight_out, shard)
    in2_over = reduce_second_over(lot2, tied(in1, out_lot1, out_lot2, out_lot3))
    lot2 = tied(lot2, in2_over)
    hiddens, d_pres = tied(((hidden1, hidden2, hidden3), (d_pre1, d_pre2, d_pre3)), in2_over)
    in2 = (cross(in2_over), *reduce_second_along(lot2))
    d_weight_out = grad_out_of((*grad1, *grad2, *grad3), hiddens)
    in3 = reduce_third(tied(lot1, d_weight_out, out_lot1, out_lot2, out_lot3), in2)
    d_weight_in = grad_in_of((*row1, *row2, *row3), tied(d_pres, in3))
    own_in = by_exp(tied(reduce_end(*in3), d_weight_in))
    rows_in = swap_exp(own_in).reshape(slots, model_width)
    out1 = reduce_first(tied(out_lot3, in3)[0])
    out_lot1, out_lot2, out1 = tied((out_lot1, out_lot2, out1), own_in)
    out2 = (cross(reduce_second_over(out_lot2, out1)), *reduce_second_along(out_lot2))
    out3 = reduce_third(out_lot1, out2)

    slope = live_mask * swish_slope(conv_out)
    d_mid, d_conv, tap_grads = conv_back_of(pick, tied(rows_in, out3), cot, slope, normed_wide, tap_count)
    own_out = reduce_end(*out3)
    expert_out = unpack(swap_exp(by_exp(own_out)).reshape(slots, model_width))
    d_conv_wide = tied(widen_rim(d_conv, half_taps), own_out)
    d_normed = jnp.zeros_like(frames_f32)
    for tap_index in range(tap_count):
        shift_at = 2 * half_taps - tap_index
        d_normed = (
            d_normed + conv_weight[tap_index] * d_conv_wide[shift_at : shift_at + frame_count]
        )
    tap_sums = sum_everywhere(tap_grads, (own_out, expert_out)).reshape(4, -1, model_width // 4)
    d_conv_weight = tap_sums.transpose(1, 0, 2).reshape(-1, model_width)[:tap_count]
    d_unit = d_normed * live_mask
    d_frames = (
        d_mid
        + inv_rms * (d_unit - unit_rows * jnp.mean(d_unit * unit_rows, axis=-1, keepdims=True))
    ).astype(BF)

    grad_out = cot.astype(F32)
    gates = (gates_local * kept_mask).T[:, :, None]
    mix_out = jnp.sum(gates * expert_out, axis=0)
    block_out = (mid_rows.astype(F32) + mix_out).astype(BF)
    d_gate_probs = kept_mask * jnp.sum(grad_out[None] * expert_out, axis=-1).T

    return (
        block_out[None],
        d_frames[None],
        d_gate_probs[None],
        d_conv_weight,
        d_weight_in,
        d_weight_out,
    )


def solution(mesh):
    in_specs = (
        P("exp", "seq", None),
        P(),
        P("exp", "seq", None),
        P("exp", "seq", None),
        P("exp"),
        P(),
        P("exp", None, "seq"),
        P("exp", "seq", None),
        P("exp", "seq", None),
    )
    out_specs = (
        P("exp", "seq", None),
        P("exp", "seq", None),
        P("exp", "seq", None),
        P(),
        P("exp", None, "seq"),
        P("exp", "seq", None),
    )
    return jax.shard_map(local, mesh=mesh, in_specs=in_specs, out_specs=out_specs, check_vma=False)
```
